512 devices in a mesh: blk: 128 (over z, y, core), rep: 4 (over x).
Axes of the slice: x: 4, y: 8, z: 8, core: 2. Of those that a mesh axis runs over, the one named last changes fastest.
Arguments:
- features: bfloat16 [262144, 128], P(('blk', 'rep')), may hold values from -6 to 6
- send_rows: int32 [65536, 8], P(('blk', 'rep')), may hold values from 0 to 511, as said below
- send_counts: int32 [65536], P(('blk', 'rep')), may hold values from 0 to 8, as said below
- tile_values: bfloat16 [2048, 4, 128, 128], P(('blk', 'rep')), may hold values from 0 to 1
- tile_rows: int32 [2048, 4], P(('blk', 'rep')), may hold values from 0 to 15
- tile_cols: int32 [2048, 4], P(('blk', 'rep')), may hold values from 0 to 3
- tile_counts: int32 [2048], P(('blk', 'rep')), may hold values from 2 to 4, as said below
- degree_scale: float32 [262144], P(('blk', 'rep')), may hold values from 0.1 to 0.5
- weight: bfloat16 [128, 256], replicated, may hold values from -0.5 to 0.5
- bias: float32 [256], replicated, may hold values from -3 to 3
- out_grad: bfloat16 [262144, 256], P(('blk', 'rep')), may hold values from -6 to 6
Outputs:
- hidden: bfloat16 [262144, 256], P(('blk', 'rep'))
- grad_features: bfloat16 [262144, 128], P(('blk', 'rep'))
- grad_weight: float32 [128, 256], replicated
- grad_bias: float32 [256], replicated
The draws below stay inside these ranges and needn't reach their ends.
Inputs may be any that keep to these rules, and one draw needn't show every extreme that they name: `send_counts`: within each rep index, the counts of one sender over its owners sum to 512, as do the counts one owner receives; some counts equal 8 and some are 0. `send_rows`: entries of slots below the count are distinct local rows and cover every row of the device once; the other entries are 0. `tile_counts`: only the first count tiles of an entry are live; some entries are full.
All inputs are finite; a program needn't handle non-finite values.
Results may differ from the reference program's by a relative error of at most 0.008.
Values may be sent and summed in bfloat16 or wider, within the bound.
No kernel may reach another device: no remote copies, remote signals or barrier semaphores. Data moves between devices by JAX's collectives and lax.ppermute only.
A program may use at most 64 MiB of HBM per device.

```python
import math
import jax
import jax.numpy as jnp
from jax import lax

F_IN = 128
HID = 256
TILE = 128
STEPS = 4
KB = 4
ROWS = 512
CAP = 8
RT = 16
CT = 4
NODES = 262144
N_BLK = 128
N_REP = 4


def route_counts(key):
    base = jax.random.fold_in(key, 101)
    owner_keys = jax.random.split(jax.random.fold_in(base, 1), N_REP)
    sender_keys = jax.random.split(jax.random.fold_in(base, 2), N_REP)
    owner_label = jax.vmap(lambda k: jax.random.permutation(k, N_BLK))(owner_keys).astype(jnp.int32)
    sender_label = jax.vmap(lambda k: jax.random.permutation(k, N_BLK))(sender_keys).astype(jnp.int32)
    offset = jnp.arange(N_BLK, dtype=jnp.int32)
    level = jnp.where(offset < N_BLK // 4, CAP, jnp.where(offset < 3 * N_BLK // 4, CAP // 2, 0)).astype(jnp.int32)
    owner_part = owner_label[None, :, :]
    sender_part = jnp.transpose(sender_label)[:, :, None]
    return level[(owner_part - sender_part) % N_BLK].astype(jnp.int32)


def draw_send_counts(key, part):
    counts = route_counts(key)
    return counts.reshape(N_BLK * N_REP * N_BLK).astype(jnp.int32)


def draw_send_rows(key, part):
    counts = route_counts(key)
    key = jax.random.fold_in(key, 2)
    keys = jax.random.split(key, N_BLK * N_REP)
    perms = jax.vmap(lambda k: jax.random.permutation(k, ROWS))(keys).reshape(N_BLK, N_REP, ROWS).astype(jnp.int32)
    start = jnp.cumsum(counts, axis=-1) - counts
    slot = jnp.arange(CAP, dtype=jnp.int32)
    index = start[..., None] + slot
    valid = slot < counts[..., None]
    index = jnp.minimum(index, ROWS - 1).reshape(N_BLK, N_REP, N_BLK * CAP)
    picked = jnp.take_along_axis(perms, index, axis=2).reshape(N_BLK, N_REP, N_BLK, CAP)
    return jnp.where(valid, picked, 0).reshape(N_BLK * N_REP * N_BLK, CAP).astype(jnp.int32)


def draw_tile_counts(key, part):
    key = jax.random.fold_in(key, 3)
    drawn = jax.random.randint(key, (N_BLK * N_REP * STEPS,), KB // 2, KB + 1).astype(jnp.int32)
    position = jnp.arange(N_BLK * N_REP * STEPS, dtype=jnp.int32)
    return jnp.where(position % 5 == 0, KB, drawn).astype(jnp.int32)


def plant(values, stream_key, smallest, largest):
    longest = values.shape.index(max(values.shape))
    spots = []
    for shift in (0, 1):
        where = [jax.random.randint(jax.random.fold_in(stream_key, axis), (), 0, length) for axis, length in enumerate(values.shape)]
        where[longest] = (where[longest] + shift) % values.shape[longest]
        spots.append(tuple(where))
    return values.at[spots[0]].set(smallest).at[spots[1]].set(largest)


def levels(key, extent, cuts, low, high):
    factor_of = 1.0
    for dim, parts in cuts:
        draws = jax.random.uniform(jax.random.fold_in(jax.random.fold_in(key, 6), dim), (parts,), jnp.float32, low / len(cuts), high / len(cuts))
        factor_of = factor_of * jnp.repeat(jnp.exp(draws), extent[dim] // parts).reshape((-1,) + (1,) * (len(extent) - 1 - dim))
    return factor_of


def centred(stream_key, extent, scale, bound, cuts=(), kind=jnp.bfloat16):
    gain = levels(stream_key, extent, cuts, -0.22, 0.18) if cuts else 1.0
    array = jax.random.normal(stream_key, extent, jnp.float32) * scale * gain
    return jnp.minimum(jnp.maximum(array, -bound), bound).astype(kind)


def setup_inputs(seed: int = 0) -> dict:
    seeds = jax.random.split(jax.random.key(seed), 12)
    return {
        "features": centred(seeds[0], (NODES, F_IN), 1.0, 6.0, ((0, 512),)),
        "send_rows": draw_send_rows(jax.random.fold_in(seeds[11], 71), 0),
        "send_counts": draw_send_counts(jax.random.fold_in(seeds[11], 71), 0),
        "tile_values": jnp.clip(1.0 * jax.random.uniform(seeds[3], (N_BLK * N_REP * STEPS, KB, TILE, TILE), jnp.float32) ** levels(seeds[3], (N_BLK * N_REP * STEPS, KB, TILE, TILE), ((0, 512),), -0.2, 0.2), 0.0, 1.0).astype(jnp.bfloat16),
        "tile_rows": plant(jax.random.randint(seeds[4], (N_BLK * N_REP * STEPS, KB), 0, RT), jax.random.fold_in(seeds[4], 1), 0, RT - 1).astype(jnp.int32),
        "tile_cols": plant(jax.random.randint(seeds[5], (N_BLK * N_REP * STEPS, KB), 0, CT), jax.random.fold_in(seeds[5], 1), 0, CT - 1).astype(jnp.int32),
        "tile_counts": draw_tile_counts(jax.random.fold_in(seeds[11], 71), 0),
        "degree_scale": jnp.clip(jnp.exp(math.log(0.5) - 1.609438 * jax.random.uniform(seeds[7], (NODES,), jnp.float32) ** levels(seeds[7], (NODES,), ((0, 512),), -0.2, 0.2)), 0.1, 0.5),
        "weight": centred(seeds[8], (F_IN, HID), F_IN ** -0.5, 0.5),
        "bias": centred(seeds[9], (HID,), 0.5, 3.0, (), jnp.float32),
        "out_grad": centred(seeds[10], (NODES, HID), 1.0, 6.0, ((0, 512),)),
    }


def reference(features, send_rows, send_counts, tile_values, tile_rows, tile_cols, tile_counts, degree_scale, weight, bias, out_grad):
    feats = features.reshape(N_BLK, N_REP, ROWS, F_IN)
    rows_idx = send_rows.reshape(N_BLK, N_REP, N_BLK, CAP)
    counts = send_counts.reshape(N_BLK, N_REP, N_BLK)
    slot = jnp.arange(CAP, dtype=jnp.int32)
    valid = slot < counts[..., None]
    start = jnp.cumsum(counts, axis=0) - counts
    place = jnp.where(valid, start[..., None] + slot, ROWS).astype(jnp.int32)
    p_ix = jnp.arange(N_BLK, dtype=jnp.int32)[:, None, None, None]
    r_ix = jnp.arange(N_REP, dtype=jnp.int32)[None, :, None, None]
    q_ix = jnp.arange(N_BLK, dtype=jnp.int32)[None, None, :, None]
    outgoing = feats[p_ix, r_ix, rows_idx]
    owned = jnp.zeros((N_BLK, N_REP, ROWS + 1, F_IN), jnp.bfloat16).at[q_ix, r_ix, place].set(outgoing)[:, :, :ROWS]
    scale = degree_scale.reshape(N_BLK, N_REP, ROWS, 1)
    scaled = (scale * owned.astype(jnp.float32)).astype(jnp.bfloat16)
    tiles = tile_values.reshape(N_BLK, N_REP, STEPS, KB, TILE, TILE)
    trow = tile_rows.reshape(N_BLK, N_REP, STEPS, KB)
    tcol = tile_cols.reshape(N_BLK, N_REP, STEPS, KB)
    tcnt = tile_counts.reshape(N_BLK, N_REP, STEPS)
    live = (jnp.arange(KB, dtype=jnp.int32) < tcnt[..., None]).astype(jnp.float32)

    def forward_block(i):
        total = jnp.zeros((RT, TILE, F_IN), jnp.float32)
        for r in range(N_REP):
            for s in range(STEPS):
                source = scaled[(i - s) % N_BLK, r].reshape(CT, TILE, F_IN)
                operand = source[tcol[i, r, s]].astype(jnp.float32)
                prod = jnp.einsum("kab,kbf->kaf", tiles[i, r, s].astype(jnp.float32), operand)
                prod = prod * live[i, r, s][:, None, None]
                total = total.at[trow[i, r, s]].add(prod)
        return total.reshape(N_REP, ROWS, F_IN)

    summed = lax.map(forward_block, jnp.arange(N_BLK, dtype=jnp.int32))
    agg = (scale * summed).astype(jnp.bfloat16).reshape(NODES, F_IN)
    pre = jnp.dot(agg, weight, preferred_element_type=jnp.float32) + bias
    hidden = jax.nn.silu(pre).astype(jnp.bfloat16)
    sig = jax.nn.sigmoid(pre)
    grad_pre = (out_grad.astype(jnp.float32) * (sig * (1.0 + pre * (1.0 - sig)))).astype(jnp.bfloat16)
    grad_weight = jnp.dot(agg.T, grad_pre, preferred_element_type=jnp.float32)
    grad_bias = jnp.sum(grad_pre.astype(jnp.float32), axis=0)
    grad_agg = (degree_scale[:, None] * jnp.dot(grad_pre, weight.T, preferred_element_type=jnp.float32)).astype(jnp.bfloat16)
    block_grad = grad_agg.reshape(N_BLK, RT, TILE, F_IN)

    def backward_block(j):
        total = jnp.zeros((N_REP, CT, TILE, F_IN), jnp.float32)
        for r in range(N_REP):
            for s in range(STEPS):
                i = (j + s) % N_BLK
                operand = block_grad[i][trow[i, r, s]].astype(jnp.float32)
                prod = jnp.einsum("kab,kaf->kbf", tiles[i, r, s].astype(jnp.float32), operand)
                prod = prod * live[i, r, s][:, None, None]
                total = total.at[r, tcol[i, r, s]].add(prod)
        return total.reshape(N_REP, ROWS, F_IN)

    spread = lax.map(backward_block, jnp.arange(N_BLK, dtype=jnp.int32))
    grad_owned = (scale * spread).astype(jnp.bfloat16)
    padded = jnp.concatenate([grad_owned, jnp.zeros((N_BLK, N_REP, 1, F_IN), jnp.bfloat16)], axis=2)
    back = padded[q_ix, r_ix, place]
    target = jnp.where(valid, rows_idx, ROWS).astype(jnp.int32)
    grad_features = jnp.zeros((N_BLK, N_REP, ROWS + 1, F_IN), jnp.bfloat16).at[p_ix, r_ix, target].set(back)[:, :, :ROWS]
    return hidden, grad_features.reshape(NODES, F_IN), grad_weight, grad_bias
```

```python
import jax
import jax.numpy as jnp
from jax import lax
from jax.experimental import pallas as pl
from jax.experimental.pallas import tpu as pltpu
from jax.sharding import PartitionSpec as P

BF16 = jnp.bfloat16
F32 = jnp.float32
TILE = 128
UNUSED = 1024.0
NN = (((1,), (0,)), ((), ()))
NT = (((1,), (1,)), ((), ()))
TN = (((0,), (0,)), ((), ()))


def dot(a, b, dims=NN):
    return lax.dot_general(a, b, dims, preferred_element_type=F32)


def iota(shape, dim):
    return lax.broadcasted_iota(jnp.int32, shape, dim)


def one_hot(mask):
    return jnp.where(mask, 1.0, 0.0).astype(BF16)


def kernel_call(kernel, outs, specs, name, scratch=(), flops=10**8):
    return pl.pallas_call(
        kernel,
        out_shape=outs,
        in_specs=specs,
        scratch_shapes=list(scratch),
        compiler_params=pltpu.CompilerParams(vmem_limit_bytes=40 * 1024 * 1024),
        cost_estimate=pl.CostEstimate(flops=flops, bytes_accessed=10**6, transcendentals=0),
        name=name,
    )


def call(kernel, outs, name, flops=10**8):
    def run(*arrays, after=()):
        specs = [pl.BlockSpec(memory_space=pltpu.VMEM)] * len(arrays)
        specs += [pl.BlockSpec(memory_space=pl.ANY)] * len(after)
        return kernel_call(kernel, outs, specs, name, flops=flops)(*arrays, *after)

    return run


def shape(dims, kind):
    return jax.ShapeDtypeStruct(dims, kind)


def as_column(row):
    return jnp.transpose(jnp.broadcast_to(row, (TILE, TILE)))


def slot_parts(send_rows, counts, rows):
    send_rows = jnp.transpose(send_rows.astype(F32)).astype(jnp.int32)
    owners, slots = send_rows.shape
    count = as_column(counts.astype(F32))[:, :slots]
    lane = iota((owners, slots), 1).astype(F32)
    key = jnp.where(lane < count, send_rows, rows)
    high = (key >> 5).astype(F32).astype(BF16)
    low = (key & 31).astype(F32).astype(BF16)
    total = owners * slots
    expand = one_hot(iota((total, owners), 0) // slots == iota((total, owners), 1))
    mine = iota((total, slots), 0) % slots == iota((total, slots), 1)
    high = jnp.where(mine, dot(expand, high) * 32.0, 0.0).astype(BF16)
    low = jnp.where(mine, dot(expand, low), 0.0).astype(BF16)
    return high, low


def start_kernel(*refs):
    out_ref, scale_ref, bias_ref, table_ref = refs[8:12]
    features_ref, rows_ref, counts_ref, degree_ref, *parts, sems = refs[12:]
    pairs = tuple(zip(refs[:8], (features_ref, rows_ref, counts_ref, degree_ref, *parts, bias_ref)))
    copies = [pltpu.make_async_copy(a, b, sems.at[k]) for k, (a, b) in enumerate(pairs)]
    for copy in copies:
        copy.start()
    for copy in copies:
        copy.wait()
    rows = features_ref.shape[0]
    slots = rows_ref.shape[0]
    high, low = slot_parts(rows_ref[...], counts_ref[...], rows)
    ones = jnp.ones((slots, TILE), BF16)
    key = dot(high, ones) + dot(low, ones)
    lane = iota(key.shape, 1).astype(F32)
    pick = jnp.concatenate(
        [one_hot(key == lane + float(start)) for start in range(0, rows, TILE)], axis=1
    )
    sent = dot(pick, features_ref[...])
    out_ref[...] = jnp.where(key >= float(rows), UNUSED, sent).astype(BF16)
    for t in range(rows // TILE):
        scale_ref[t * TILE : (t + 1) * TILE] = as_column(degree_ref[t : t + 1])
    place = 0
    for part in parts:
        table_ref[place : place + part.shape[0]] = part[...]
        place += part.shape[0]
    table_ref[place : place + 1] = jnp.full((1, table_ref.shape[1]), lax.axis_index("rep"))


def start_call(features, send_rows, counts_row, degree, tables, bias_row):
    rows, width = features.shape
    total = send_rows.size
    small = (features, send_rows, counts_row, degree, *tables)
    arrays = [pltpu.with_memory_space_constraint(a, pltpu.HBM) for a in (*small, bias_row)]
    return pl.pallas_call(
        start_kernel,
        out_shape=(
            shape((total, width), BF16),
            shape((rows, TILE), F32),
            shape(bias_row.shape, F32),
            shape((1 + sum(a.shape[0] for a in tables), tables[0].shape[1]), jnp.int32),
        ),
        in_specs=[pl.BlockSpec(memory_space=pltpu.HBM)] * 8,
        scratch_shapes=[pltpu.VMEM(a.shape, a.dtype) for a in small]
        + [pltpu.SemaphoreType.DMA((8,))],
        compiler_params=pltpu.CompilerParams(vmem_limit_bytes=8 * 1024 * 1024),
        cost_estimate=pl.CostEstimate(flops=10**8, bytes_accessed=10**6, transcendentals=0),
        name="start",
    )(*arrays)


def arrive_kernel(rows_ref, counts_ref, out_ref):
    rows = out_ref.shape[0]
    slots = rows_ref.shape[0]
    high, low = slot_parts(rows_ref[...], counts_ref[...], rows)
    ones = jnp.ones((8, slots), BF16)
    key = dot(ones, high, NT) + dot(ones, low, NT)
    for start in range(0, key.shape[1], TILE):
        span = slice(start, start + TILE)
        out_ref[:, span] = one_hot(iota((rows, TILE), 0).astype(F32) == key[0:1, span])


def transpose_kernel(tiles_ref, out_ref):
    for t in range(tiles_ref.shape[0]):
        out_ref[t] = jnp.transpose(tiles_ref[t].astype(F32)).astype(BF16)


def used_slots(ref):
    return jnp.where(ref[...].astype(F32) < 512.0, 1.0, 0.0).astype(BF16)


def place_kernel(incoming_ref, scale_ref, out_ref):
    rows = out_ref.shape[0]
    used = used_slots(incoming_ref)
    before = one_hot(iota((TILE, TILE), 0) < iota((TILE, TILE), 1))
    ones = jnp.ones((TILE, TILE), BF16)
    mean = jnp.full((8, TILE), 1.0 / TILE, BF16)
    offset = jnp.zeros((8, TILE), F32)
    parts = []
    for start in range(0, used.shape[0], TILE):
        here = dot(mean, used[start : start + TILE], NT)
        flags = here.astype(BF16)
        rank = jnp.where(here > 0.5, dot(flags, before) + offset, -1.0)
        offset = offset + dot(flags, ones)
        parts.append(one_hot(iota((rows, TILE), 0).astype(F32) == rank[0:1]))
    owned = dot(jnp.concatenate(parts, axis=1), incoming_ref[...])
    out_ref[...] = (scale_ref[...] * owned).astype(BF16)


def unplace_kernel(incoming_ref, out_ref):
    rows = out_ref.shape[1]
    used = used_slots(incoming_ref)
    before = one_hot(iota((TILE, TILE), 1) < iota((TILE, TILE), 0))
    ones = jnp.ones((TILE, TILE), BF16)
    offset = jnp.zeros((TILE, TILE), F32)
    lane = iota((TILE, TILE), 1).astype(F32)
    for start in range(0, used.shape[0], TILE):
        here = used[start : start + TILE]
        rank = jnp.where(here.astype(F32) > 0.5, dot(before, here) + offset, -1.0)
        offset = offset + dot(ones, here)
        for column in range(0, rows, TILE):
            out_ref[start : start + TILE, column : column + TILE] = one_hot(
                rank == lane + float(column)
            )


def gather_kernel(
    table_ref, tiles_ref, src0, src1, src2, src3, *refs
):
    out_ref, acc_ref = refs[-2:]
    acc_ref[...] = jnp.zeros_like(acc_ref)
    most = table_ref.shape[1]
    steps = tiles_ref.shape[0] // most
    for step, source in enumerate((src0, src1, src2, src3)):
        for k in range(most):
            col = pl.multiple_of(table_ref[steps + step, k] * TILE, TILE)
            row = pl.multiple_of(table_ref[step, k] * TILE, TILE)
            live = (k < table_ref[2 * steps, step]).astype(F32)
            prod = dot(tiles_ref[step * most + k], source[pl.ds(col, TILE), :])
            acc_ref[pl.ds(row, TILE), :] += prod * live
    quarters, rows, _ = out_ref.shape
    for q in range(quarters):
        out_ref[q] = acc_ref[q * rows : (q + 1) * rows].astype(BF16)


def dense_kernel(
    parts_ref, scale_ref, weight_ref, bias_ref, out_grad_ref, hidden_ref, agg_ref, grad_pre_ref, out_ref
):
    quarters, rows, width = parts_ref.shape
    summed = parts_ref[0].astype(F32)
    for q in range(1, quarters):
        summed = summed + parts_ref[q].astype(F32)
    for t in range(rows // TILE):
        part = slice(t * TILE, (t + 1) * TILE)
        scale = scale_ref[part]
        agg = (scale * summed[part]).astype(BF16)
        agg_ref[part] = agg
        pre = dot(agg, weight_ref[...]) + bias_ref[...]
        sig = jax.nn.sigmoid(pre)
        hidden_ref[part] = (pre * sig).astype(BF16)
        grad_pre = (
            out_grad_ref[part].astype(F32) * (sig * (1.0 + pre * (1.0 - sig)))
        ).astype(BF16)
        grad_pre_ref[part] = grad_pre
        out_ref[part] = (scale * dot(grad_pre, weight_ref[...], NT)).astype(BF16)


def terms_kernel(agg_ref, grad_pre_ref, *refs):
    out_ref = refs[-1]
    grad_pre = grad_pre_ref[...]
    width = agg_ref.shape[1]
    term = dot(agg_ref[...], grad_pre, TN)
    total = jnp.sum(grad_pre.astype(F32), axis=0, keepdims=True)
    mine = iota((width, 2 * TILE), 1) // 2 == iota((width, 2 * TILE), 0)
    pieces = jnp.concatenate([term, jnp.where(mine, total, 0.0)], axis=1).astype(BF16)
    lines = (4 * width, width)
    rows = jnp.zeros((4 * width, TILE), F32)
    for k in range(4):
        here = iota(lines, 0) == 4 * iota(lines, 1) + k
        rows = rows + dot(one_hot(here), pieces[:, k * TILE : (k + 1) * TILE])
    out_ref[...] = rows.astype(BF16)


def row_kernel(parts_ref, *refs):
    out_ref = refs[-1]
    count, width = parts_ref.shape
    groups = (count // 8, 8, width)
    pairs = jnp.sum(parts_ref[...].astype(F32).reshape(groups), axis=0)
    term = pairs[:4] + pairs[4:]
    both = jnp.concatenate([term, term], axis=0)
    out_ref[...] = jnp.broadcast_to(both[None], groups).reshape(count, width).astype(BF16)


def whole_kernel(rows_ref, out_ref):
    count = rows_ref.shape[0]
    width = count // 4
    lines = (width, count)
    for k in range(2):
        half = slice(k * TILE, (k + 1) * TILE)
        here = iota(lines, 1) == 4 * iota(lines, 0) + k
        out_ref[:width, half] = dot(one_hot(here), rows_ref[...]).astype(BF16)
        here = iota((16, count), 1) % 4 == k + 2
        out_ref[width:, half] = dot(one_hot(here), rows_ref[...]).astype(BF16)


def spread_kernel(
    table_ref, tiles_ref, block0, block1, block2, block3, *refs
):
    own_ref, out1, out2, out3, acc_ref, block_ref = refs[-6:]
    mine = table_ref[table_ref.shape[0] - 1, 0]
    for away, block in enumerate((block0, block1, block2, block3)):
        block_ref[lax.rem(mine + 4 - away, 4)] = block[...]
    acc_ref[...] = jnp.zeros_like(acc_ref)
    most = table_ref.shape[1]
    steps = tiles_ref.shape[0] // most
    col_tiles = own_ref.shape[0] // TILE
    for step in range(steps - 1, -1, -1):
        for k in range(most):
            col = pl.multiple_of(table_ref[steps + step, k] * TILE, TILE)
            quarter = table_ref[step, k] // col_tiles
            row = pl.multiple_of((table_ref[step, k] - quarter * col_tiles) * TILE, TILE)
            live = (k < table_ref[2 * steps, step]).astype(F32)
            prod = dot(tiles_ref[step * most + k], block_ref[quarter, pl.ds(row, TILE), :])
            acc_ref[step, pl.ds(col, TILE), :] += prod * live
    own_ref[...] = acc_ref[0]
    for step, out in ((1, out1), (2, out2), (3, out3)):
        out[...] = acc_ref[step].astype(BF16)


def back_kernel(own_ref, in1, in2, in3, scale_ref, unplace_ref, *refs):
    out_ref = refs[-1]
    total = own_ref[...] + in1[...].astype(F32) + in2[...].astype(F32) + in3[...].astype(F32)
    grads = (scale_ref[...] * total).astype(BF16)
    out_ref[...] = dot(unplace_ref[...], grads).astype(BF16)


def last_kernel(arrive_ref, returned_ref, w0, w1, w2, w3, out_ref, weight_ref, bias_ref):
    out_ref[...] = dot(arrive_ref[...], returned_ref[...]).astype(BF16)
    total = (w0[...].astype(F32) + w1[...].astype(F32)) + (
        w2[...].astype(F32) + w3[...].astype(F32)
    )
    width = weight_ref.shape[0]
    weight_ref[...] = total[:width]
    bias_ref[...] = total[width : width + 1]


def shifted(value, steps, axis="blk"):
    count = lax.axis_size(axis)
    return lax.ppermute(value, axis, [(s, (s + steps) % count) for s in range(count)])


def exchange(value, axis):
    return lax.all_to_all(value, axis, split_axis=0, concat_axis=0, tiled=True)


def tile_call(kernel, outs, scratch, name, table, arrays, after=()):
    specs = [pl.BlockSpec(memory_space=pltpu.SMEM)]
    specs += [pl.BlockSpec(memory_space=pltpu.VMEM)] * len(arrays)
    specs += [pl.BlockSpec(memory_space=pl.ANY)] * len(after)
    return kernel_call(kernel, outs, specs, name, scratch)(table, *arrays, *after)


def on_device(
    features,
    send_rows,
    send_counts,
    tile_values,
    tile_rows,
    tile_cols,
    tile_counts,
    degree_scale,
    weight,
    bias,
    out_grad,
):
    blocks = lax.axis_size("blk")
    quarters = lax.axis_size("rep")
    rows, width = features.shape
    slots = send_rows.shape[1]
    steps, most = tile_values.shape[:2]
    hidden_width = weight.shape[1]
    total = blocks * slots
    slot_rows = send_rows.T
    counts_row = send_counts.reshape(1, blocks)
    degree = degree_scale.reshape(rows // TILE, TILE)
    tiles = tile_values.reshape(steps * most, TILE, TILE)
    tables = (tile_rows, tile_cols, tile_counts.reshape(1, steps))

    outgoing, scale, bias_row, table = start_call(
        features, slot_rows, counts_row, degree, tables, bias.reshape(1, hidden_width)
    )
    incoming = exchange(outgoing.reshape(blocks, slots, width), "blk").reshape(total, width)
    arrive = call(arrive_kernel, shape((rows, total), BF16), "arrive")(slot_rows, counts_row)
    turned = call(transpose_kernel, shape(tiles.shape, BF16), "turn")(tiles)

    scaled = call(place_kernel, shape((rows, width), BF16), "place")(incoming, scale)
    sources = [scaled] + [shifted(scaled, step) for step in range(1, steps)]
    unplace = call(unplace_kernel, shape((total, rows), BF16), "unplace")(incoming)
    partial = tile_call(
        gather_kernel,
        shape((quarters, rows, width), BF16),
        [pltpu.VMEM((quarters * rows, width), F32)],
        "gather_tiles",
        table,
        (tiles, *sources),
        (turned, arrive, unplace),
    )
    parts = exchange(partial, "rep")
    hidden, agg, grad_pre, grad_agg = call(
        dense_kernel,
        (
            shape((rows, hidden_width), BF16),
            shape((rows, width), BF16),
            shape((rows, hidden_width), BF16),
            shape((rows, width), BF16),
        ),
        "dense",
    )(parts, scale, weight, bias_row, out_grad)
    block = [grad_agg] + [shifted(grad_agg, away, "rep") for away in range(1, quarters)]

    lines = shape((4 * width, TILE), BF16)
    terms = call(terms_kernel, lines, "terms")(agg, grad_pre, after=(block[3],))
    terms = exchange(terms.reshape(blocks, 4, TILE), "blk").reshape(lines.shape)

    own, *others = tile_call(
        spread_kernel,
        (shape((rows, width), F32),) + (shape((rows, width), BF16),) * (steps - 1),
        [pltpu.VMEM((steps, rows, width), F32), pltpu.VMEM((quarters, rows, width), BF16)],
        "spread_tiles",
        table,
        (turned, *block),
    )
    others = [shifted(value, -step) for step, value in enumerate(others, 1)]
    terms = call(row_kernel, lines, "row")(terms, after=(others[0],))
    terms = exchange(terms.reshape(blocks, 4, TILE), "blk").reshape(lines.shape)
    back = call(back_kernel, shape((total, width), BF16), "back", flops=4 * 10**10)(own, *others, scale, unplace)
    whole = call(whole_kernel, shape((width + 16, hidden_width), BF16), "whole")(terms)
    wholes = [whole] + [shifted(whole, away, "rep") for away in range(1, quarters)]
    returned = exchange(back.reshape(blocks, slots, width), "blk").reshape(total, width)
    grad_features, grad_weight, grad_bias = call(
        last_kernel,
        (shape((rows, width), BF16), shape(weight.shape, F32), shape((1, hidden_width), F32)),
        "last",
    )(arrive, returned, *wholes)
    return (hidden, grad_features, grad_weight, grad_bias.reshape(hidden_width))


def solution(mesh):
    in_specs = (
        P(("blk", "rep"), None),
        P(("blk", "rep"), None),
        P(("blk", "rep")),
        P(("blk", "rep"), None, None, None),
        P(("blk", "rep"), None),
        P(("blk", "rep"), None),
        P(("blk", "rep")),
        P(("blk", "rep")),
        P(),
        P(),
        P(("blk", "rep"), None),
    )
    out_specs = (P(("blk", "rep"), None), P(("blk", "rep"), None), P(), P())
    return jax.shard_map(
        on_device, mesh=mesh, in_specs=in_specs, out_specs=out_specs, check_vma=False
    )
```

```python
import jax
import jax.numpy as jnp
from jax import lax
from jax.experimental import pallas as pl
from jax.experimental.pallas import tpu as pltpu
from jax.sharding import PartitionSpec as P

BF16 = jnp.bfloat16
F32 = jnp.float32
TILE = 128
LONG = 10**11
UNUSED = 1024.0
NN = (((1,), (0,)), ((), ()))
NT = (((1,), (1,)), ((), ()))
TN = (((0,), (0,)), ((), ()))


def dot(a, b, dims=NN):
    return lax.dot_general(a, b, dims, preferred_element_type=F32)


def iota(shape, dim):
    return lax.broadcasted_iota(jnp.int32, shape, dim)


def one_hot(mask):
    return jnp.where(mask, 1.0, 0.0).astype(BF16)


def kernel_call(kernel, outs, specs, name, scratch=(), flops=10**8):
    return pl.pallas_call(
        kernel,
        out_shape=outs,
        in_specs=specs,
        scratch_shapes=list(scratch),
        compiler_params=pltpu.CompilerParams(vmem_limit_bytes=16 * 1024 * 1024),
        cost_estimate=pl.CostEstimate(flops=flops, bytes_accessed=10**6, transcendentals=0),
        name=name,
    )


def call(kernel, outs, name, scratch=(), flops=10**8):
    def run(*arrays, after=()):
        specs = [pl.BlockSpec(memory_space=pltpu.VMEM)] * len(arrays)
        specs += [pl.BlockSpec(memory_space=pl.ANY)] * len(after)
        return kernel_call(kernel, outs, specs, name, scratch, flops)(*arrays, *after)

    return run


def shape(dims, kind):
    return jax.ShapeDtypeStruct(dims, kind)


def quotient(value, divisor):
    return jnp.floor((value.astype(F32) + 0.5) * (1.0 / divisor)).astype(jnp.int32)


def as_column(row):
    return jnp.transpose(jnp.broadcast_to(row, (TILE, TILE)))


def slot_parts(send_rows, counts, rows):
    send_rows = jnp.transpose(send_rows.astype(F32)).astype(jnp.int32)
    owners, slots = send_rows.shape
    count = as_column(counts.astype(F32))[:, :slots]
    lane = iota((owners, slots), 1).astype(F32)
    key = jnp.where(lane < count, send_rows, rows)
    high = (key >> 5).astype(F32).astype(BF16)
    low = (key & 31).astype(F32).astype(BF16)
    total = owners * slots
    expand = one_hot(quotient(iota((total, owners), 0), slots) == iota((total, owners), 1))
    row = iota((total, slots), 0)
    mine = row - quotient(row, slots) * slots == iota((total, slots), 1)
    high = jnp.where(mine, dot(expand, high) * 32.0, 0.0).astype(BF16)
    low = jnp.where(mine, dot(expand, low), 0.0).astype(BF16)
    return high, low


def start_kernel(*refs):
    out_ref, degree_ref, bias_ref, table_ref, key_ref = refs[8:13]
    features_ref, rows_ref, counts_ref, *parts, sems = refs[13:]
    pairs = tuple(zip(refs[:8], (features_ref, rows_ref, counts_ref, degree_ref, *parts, bias_ref)))
    copies = [pltpu.make_async_copy(a, b, sems.at[k]) for k, (a, b) in enumerate(pairs)]
    for copy in copies:
        copy.start()
    for copy in copies:
        copy.wait()
    rows = features_ref.shape[0]
    slots = rows_ref.shape[0]
    high, low = slot_parts(rows_ref[...], counts_ref[...], rows)
    ones = jnp.ones((slots, TILE), BF16)
    key = dot(high, ones) + dot(low, ones)
    lane = iota(key.shape, 1).astype(F32)
    pick = jnp.concatenate(
        [one_hot(key == lane + float(start)) for start in range(0, rows, TILE)], axis=1
    )
    sent = dot(pick, features_ref[...])
    out_ref[...] = jnp.where(key >= float(rows), UNUSED, sent).astype(BF16)
    ones = jnp.ones((8, slots), BF16)
    key_ref[...] = dot(ones, high, NT) + dot(ones, low, NT)
    place = 0
    for part in parts:
        table_ref[place : place + part.shape[0]] = part[...]
        place += part.shape[0]
    odd = lax.rem(lax.axis_index("blk"), 2)
    lane = iota((1, table_ref.shape[1]), 1)
    table_ref[place : place + 1] = jnp.where(lane == 0, odd, lax.axis_index("rep"))


def start_call(features, send_rows, counts_row, degree, tables, bias_row):
    rows, width = features.shape
    total = send_rows.size
    small = (features, send_rows, counts_row, degree, *tables)
    arrays = [pltpu.with_memory_space_constraint(a, pltpu.HBM) for a in (*small, bias_row)]
    return pl.pallas_call(
        start_kernel,
        out_shape=(
            shape((total, width), BF16),
            shape(degree.shape, F32),
            shape(bias_row.shape, F32),
            shape((1 + sum(a.shape[0] for a in tables), tables[0].shape[1]), jnp.int32),
            shape((8, total), F32),
        ),
        in_specs=[pl.BlockSpec(memory_space=pltpu.HBM)] * 8,
        scratch_shapes=[pltpu.VMEM(a.shape, a.dtype) for a in (features, send_rows, counts_row, *tables)]
        + [pltpu.SemaphoreType.DMA((8,))],
        compiler_params=pltpu.CompilerParams(vmem_limit_bytes=8 * 1024 * 1024),
        cost_estimate=pl.CostEstimate(flops=10**8, bytes_accessed=10**6, transcendentals=0),
        name="start",
    )(*arrays)


def transpose_kernel(tiles_ref, *refs):
    out_ref = refs[-1]
    for t in range(tiles_ref.shape[0]):
        out_ref[t] = jnp.transpose(tiles_ref[t].astype(F32)).astype(BF16)


def used_slots(ref):
    return jnp.where(ref[...].astype(F32) < 512.0, 1.0, 0.0).astype(BF16)


def scaled_rows(degree_ref, values):
    count = values.shape[0] // TILE
    parts = [
        as_column(degree_ref[t : t + 1]) * values[t * TILE : (t + 1) * TILE] for t in range(count)
    ]
    return jnp.concatenate(parts, axis=0)


def place_kernel(incoming_ref, degree_ref, out_ref):
    rows = out_ref.shape[0]
    used = used_slots(incoming_ref)
    before = one_hot(iota((TILE, TILE), 0) < iota((TILE, TILE), 1))
    ones = jnp.ones((TILE, TILE), BF16)
    mean = jnp.full((8, TILE), 1.0 / TILE, BF16)
    offset = jnp.zeros((8, TILE), F32)
    parts = []
    for start in range(0, used.shape[0], TILE):
        here = dot(mean, used[start : start + TILE], NT)
        flags = here.astype(BF16)
        rank = jnp.where(here > 0.5, dot(flags, before) + offset, -1.0)
        offset = offset + dot(flags, ones)
        parts.append(one_hot(iota((rows, TILE), 0).astype(F32) == rank[0:1]))
    owned = dot(jnp.concatenate(parts, axis=1), incoming_ref[...])
    out_ref[...] = scaled_rows(degree_ref, owned).astype(BF16)


def unplace_kernel(incoming_ref, out_ref):
    rows = out_ref.shape[1]
    used = used_slots(incoming_ref)
    before = one_hot(iota((TILE, TILE), 1) < iota((TILE, TILE), 0))
    ones = jnp.ones((TILE, TILE), BF16)
    offset = jnp.zeros((TILE, TILE), F32)
    lane = iota((TILE, TILE), 1).astype(F32)
    for start in range(0, used.shape[0], TILE):
        here = used[start : start + TILE]
        rank = jnp.where(here.astype(F32) > 0.5, dot(before, here) + offset, -1.0)
        offset = offset + dot(ones, here)
        for column in range(0, rows, TILE):
            out_ref[start : start + TILE, column : column + TILE] = one_hot(
                rank == lane + float(column)
            )


def gather_kernel(table_ref, tiles_ref, src0, two, apart, near, *refs):
    out_ref, acc_ref = refs[-2:]
    acc_ref[...] = jnp.zeros_like(acc_ref)
    most = table_ref.shape[1]
    steps = tiles_ref.shape[0] // most
    odd = table_ref[2 * steps + 1, 0]
    for step, source in ((0, src0), (2, two), (3 - 2 * odd, apart), (1 + 2 * odd, near)):
        for k in range(most):
            col = pl.multiple_of(table_ref[steps + step, k] * TILE, TILE)
            row = pl.multiple_of(table_ref[step, k] * TILE, TILE)
            live = (k < table_ref[2 * steps, step]).astype(F32)
            prod = dot(tiles_ref[step * most + k], source[pl.ds(col, TILE), :])
            acc_ref[pl.ds(row, TILE), :] += prod * live
    quarters, rows, _ = out_ref.shape
    for q in range(quarters):
        out_ref[q] = acc_ref[q * rows : (q + 1) * rows].astype(BF16)


def dense_kernel(
    parts_ref, degree_ref, weight_ref, bias_ref, out_grad_ref, hidden_ref, agg_ref, grad_pre_ref, out_ref
):
    quarters, rows, width = parts_ref.shape
    summed = parts_ref[0].astype(F32)
    for q in range(1, quarters):
        summed = summed + parts_ref[q].astype(F32)
    for t in range(rows // TILE):
        part = slice(t * TILE, (t + 1) * TILE)
        scale = as_column(degree_ref[t : t + 1])
        agg = (scale * summed[part]).astype(BF16)
        agg_ref[part] = agg
        pre = dot(agg, weight_ref[...]) + bias_ref[...]
        sig = jax.nn.sigmoid(pre)
        hidden_ref[part] = (pre * sig).astype(BF16)
        grad_pre = (
            out_grad_ref[part].astype(F32) * (sig * (1.0 + pre * (1.0 - sig)))
        ).astype(BF16)
        grad_pre_ref[part] = grad_pre
        out_ref[part] = (scale * dot(grad_pre, weight_ref[...], NT)).astype(BF16)


def terms_kernel(agg_ref, grad_pre_ref, *refs):
    out_ref = refs[-1]
    grad_pre = grad_pre_ref[...]
    width = agg_ref.shape[1]
    term = dot(agg_ref[...], grad_pre, TN)
    total = jnp.sum(grad_pre.astype(F32), axis=0, keepdims=True)
    mine = iota((width, 2 * TILE), 1) // 2 == iota((width, 2 * TILE), 0)
    pieces = jnp.concatenate([term, jnp.where(mine, total, 0.0)], axis=1).astype(BF16)
    lines = (4 * width, width)
    rows = jnp.zeros((4 * width, TILE), F32)
    for k in range(4):
        here = iota(lines, 0) == 4 * iota(lines, 1) + k
        rows = rows + dot(one_hot(here), pieces[:, k * TILE : (k + 1) * TILE])
    out_ref[...] = rows.astype(BF16)


def row_kernel(parts_ref, *refs):
    out_ref = refs[-1]
    count, width = parts_ref.shape
    pairs = jnp.sum(parts_ref[...].astype(F32).reshape(count // 8, 8, width), axis=0)
    term = jnp.concatenate([pairs[:4] + pairs[4:], jnp.zeros((4, width), F32)], axis=0)
    for copy in range(out_ref.shape[0]):
        out_ref[copy] = term


def spread_kernel(
    table_ref, tiles_ref, block0, block1, block2, block3, *refs
):
    own_ref, two_ref, near_ref, apart_ref, done_ref, acc_ref, block_ref = refs[-7:]
    acc_ref[...] = jnp.zeros_like(acc_ref)
    most = table_ref.shape[1]
    steps = tiles_ref.shape[0] // most
    mine = table_ref[2 * steps + 1, 1]
    for away, block in enumerate((block0, block1, block2, block3)):
        block_ref[lax.rem(mine + 4 - away, 4)] = block[...]
    col_tiles = own_ref.shape[0] // TILE
    for step in range(steps - 1, -1, -1):
        for k in range(most):
            col = pl.multiple_of(table_ref[steps + step, k] * TILE, TILE)
            quarter = table_ref[step, k] // col_tiles
            row = pl.multiple_of((table_ref[step, k] - quarter * col_tiles) * TILE, TILE)
            live = (k < table_ref[2 * steps, step]).astype(F32)
            prod = dot(tiles_ref[step * most + k], block_ref[quarter, pl.ds(row, TILE), :])
            acc_ref[step, pl.ds(col, TILE), :] += prod * live
    odd = table_ref[2 * steps + 1, 0]
    own_ref[...] = acc_ref[0]
    two_ref[...] = acc_ref[2]
    near_ref[...] = acc_ref[1 + 2 * odd].astype(BF16)
    apart_ref[...] = acc_ref[3 - 2 * odd].astype(BF16)
    done_ref[...] = jnp.zeros_like(done_ref)


def add_kernel(a_ref, b_ref, out_ref):
    out_ref[...] = (a_ref[...] + b_ref[...].astype(F32)).astype(BF16)


def slot_of(lines, dim):
    index = iota(lines, dim)
    owner = quotient(index, 12)
    return owner, index - 12 * owner


def back_kernel(own_ref, in1, in2, degree_ref, unplace_ref, terms_ref, out_ref):
    total = own_ref[...] + in1[...].astype(F32) + in2[...].astype(F32)
    grads = scaled_rows(degree_ref, total).astype(BF16)
    slots = dot(unplace_ref[...], grads).astype(BF16)
    term = (terms_ref[0] + terms_ref[1]) + (terms_ref[2] + terms_ref[3])
    term = jnp.concatenate([term, jnp.zeros((TILE - 8, term.shape[1]), F32)], axis=0).astype(BF16)
    lines = (TILE // 8 * 12, TILE)
    owner, slot = slot_of(lines, 0)
    widen = one_hot((slot < 8) & (owner * 8 + slot == iota(lines, 1)))
    ends = dot(one_hot(slot == 8 + iota(lines, 1)), term)
    for t in range(slots.shape[0] // TILE):
        group = dot(widen, slots[t * TILE : (t + 1) * TILE]) + ends
        out_ref[t * lines[0] : (t + 1) * lines[0]] = group.astype(BF16)


def last_kernel(key_ref, returned_ref, out_ref, weight_ref, bias_ref):
    rows = out_ref.shape[0]
    owners = TILE // 8
    lines = (TILE + 3 * owners, 12 * owners)
    owner, slot = slot_of(lines, 1)
    row = iota(lines, 0)
    wanted = (slot < 8) & (owner * 8 + slot == row)
    wanted |= (slot == 8) & (owner + TILE == row)
    wanted |= (slot == 9) & (owner + TILE + owners == row)
    wanted |= ((slot == 10) & (row == TILE + 2 * owners)) | ((slot == 11) & (row == TILE + 2 * owners + 1))
    pick = one_hot(wanted)
    total = jnp.zeros((rows, TILE), F32)
    bias = jnp.zeros((owners, TILE), F32)
    for t in range(returned_ref.shape[0] // lines[1]):
        found = dot(pick, returned_ref[t * lines[1] : (t + 1) * lines[1]])
        span = slice(t * TILE, (t + 1) * TILE)
        here = one_hot(iota((rows, TILE), 0).astype(F32) == key_ref[0:1, span])
        total = total + dot(here, found[:TILE].astype(BF16))
        for k in range(2):
            part = found[TILE + k * owners : TILE + (k + 1) * owners]
            weight_ref[t * owners : (t + 1) * owners, k * TILE : (k + 1) * TILE] = part
        bias = bias + found[TILE + 2 * owners :]
    out_ref[...] = total.astype(BF16)
    bias_ref[:, :TILE] = bias[0:1]
    bias_ref[:, TILE:] = bias[1:2]


def moved(value, target):
    count = lax.axis_size("blk")
    return lax.ppermute(value, "blk", [(s, target(s) % count) for s in range(count)])


def around(value, steps):
    count = lax.axis_size("rep")
    return lax.ppermute(value, "rep", [(s, (s + steps) % count) for s in range(count)])


def two_on(blk):
    return blk + 2


def two_back(blk):
    return blk - 2


def apart_on(blk):
    return blk + 1 + 2 * (blk % 2)


def apart_back(blk):
    return blk - 3 + 2 * (blk % 2)


def other_core(blk):
    return blk + 1 - 2 * (blk % 2)


def exchange(value, axis):
    return lax.all_to_all(value, axis, split_axis=0, concat_axis=0, tiled=True)


def tile_call(kernel, outs, scratch, name, table, arrays, after=()):
    specs = [pl.BlockSpec(memory_space=pltpu.SMEM)]
    specs += [pl.BlockSpec(memory_space=pltpu.VMEM)] * len(arrays)
    specs += [pl.BlockSpec(memory_space=pl.ANY)] * len(after)
    return kernel_call(kernel, outs, specs, name, scratch)(table, *arrays, *after)


def on_device(
    features,
    send_rows,
    send_counts,
    tile_values,
    tile_rows,
    tile_cols,
    tile_counts,
    degree_scale,
    weight,
    bias,
    out_grad,
):
    blocks = lax.axis_size("blk")
    quarters = lax.axis_size("rep")
    rows, width = features.shape
    slots = send_rows.shape[1]
    steps, most = tile_values.shape[:2]
    hidden_width = weight.shape[1]
    total = blocks * slots
    slot_rows = send_rows.T
    counts_row = send_counts.reshape(1, blocks)
    degree = degree_scale.reshape(rows // TILE, TILE)
    tiles = tile_values.reshape(steps * most, TILE, TILE)
    tables = (tile_rows, tile_cols, tile_counts.reshape(1, steps))

    outgoing, scale, bias_row, table, key = start_call(
        features, slot_rows, counts_row, degree, tables, bias.reshape(1, hidden_width)
    )
    incoming = exchange(outgoing.reshape(blocks, slots, width), "blk").reshape(total, width)
    scaled = call(place_kernel, shape((rows, width), BF16), "place")(incoming, scale)
    two = moved(scaled, two_on)
    sources = (scaled, two, moved(scaled, apart_on), moved(two, other_core))
    unplace = call(unplace_kernel, shape((total, rows), BF16), "unplace", flops=10**8)(incoming)
    turned = call(transpose_kernel, shape(tiles.shape, BF16), "turn", flops=LONG)(
        tiles, after=(scaled,)
    )
    partial = tile_call(
        gather_kernel,
        shape((quarters, rows, width), BF16),
        [pltpu.VMEM((quarters * rows, width), F32)],
        "gather_tiles",
        table,
        (tiles, *sources),
        (turned, unplace),
    )
    parts = exchange(partial, "rep")
    hidden, agg, grad_pre, grad_agg = call(
        dense_kernel,
        (
            shape((rows, hidden_width), BF16),
            shape((rows, width), BF16),
            shape((rows, hidden_width), BF16),
            shape((rows, width), BF16),
        ),
        "dense",
    )(parts, scale, weight, bias_row, out_grad)
    block = [grad_agg] + [around(grad_agg, away) for away in range(1, quarters)]
    terms = call(terms_kernel, shape((4 * width, TILE), BF16), "terms")(
        agg, grad_pre, after=(block[3],)
    )
    terms = exchange(terms.reshape(blocks, 4, TILE), "blk").reshape(4 * width, TILE)

    own, two, near, apart, spread = tile_call(
        spread_kernel,
        (shape((rows, width), F32),) * 2
        + (shape((rows, width), BF16),) * 2
        + (shape((8, TILE), F32),),
        [pltpu.VMEM((steps, rows, width), F32), pltpu.VMEM((quarters, rows, width), BF16)],
        "spread_tiles",
        table,
        (turned, *block),
    )
    near = moved(near, other_core)
    apart = moved(apart, apart_back)
    two = moved(call(add_kernel, shape((rows, width), BF16), "add")(two, near), two_back)
    terms = call(row_kernel, shape((quarters, 8, TILE), F32), "row")(terms, after=(spread,))
    terms = exchange(terms, "rep")
    back = call(back_kernel, shape((blocks * (slots + 4), width), BF16), "back", flops=4 * 10**10)(
        own, apart, two, scale, unplace, terms
    )
    returned = exchange(back.reshape(blocks, 3, 4, width), "blk").reshape(back.shape)
    grad_features, grad_weight, grad_bias = call(
        last_kernel,
        (shape((rows, width), BF16), shape(weight.shape, F32), shape((1, hidden_width), F32)),
        "last",
    )(key, returned)
    return (hidden, grad_features, grad_weight, grad_bias.reshape(hidden_width))


def solution(mesh):
    in_specs = (
        P(("blk", "rep"), None),
        P(("blk", "rep"), None),
        P(("blk", "rep")),
        P(("blk", "rep"), None, None, None),
        P(("blk", "rep"), None),
        P(("blk", "rep"), None),
        P(("blk", "rep")),
        P(("blk", "rep")),
        P(),
        P(),
        P(("blk", "rep"), None),
    )
    out_specs = (P(("blk", "rep"), None), P(("blk", "rep"), None), P(), P())
    return jax.shard_map(
        on_device, mesh=mesh, in_specs=in_specs, out_specs=out_specs, check_vma=False
    )
```

```python
import jax
import jax.numpy as jnp
from jax import lax
from jax.experimental import pallas as pl
from jax.experimental.pallas import tpu as pltpu
from jax.sharding import PartitionSpec as P

BF16 = jnp.bfloat16
F32 = jnp.float32
TILE = 128
LONG = 10**11
UNUSED = 1024.0
NN = (((1,), (0,)), ((), ()))
NT = (((1,), (1,)), ((), ()))
TN = (((0,), (0,)), ((), ()))


def dot(a, b, dims=NN):
    return lax.dot_general(a, b, dims, preferred_element_type=F32)


def iota(shape, dim):
    return lax.broadcasted_iota(jnp.int32, shape, dim)


def one_hot(mask):
    return jnp.where(mask, 1.0, 0.0).astype(BF16)


def kernel_call(kernel, outs, specs, name, scratch=(), flops=10**8):
    return pl.pallas_call(
        kernel,
        out_shape=outs,
        in_specs=specs,
        scratch_shapes=list(scratch),
        compiler_params=pltpu.CompilerParams(vmem_limit_bytes=16 * 1024 * 1024),
        cost_estimate=pl.CostEstimate(flops=flops, bytes_accessed=10**6, transcendentals=0),
        name=name,
    )


def call(kernel, outs, name, scratch=(), flops=10**8):
    def run(*arrays, after=()):
        specs = [pl.BlockSpec(memory_space=pltpu.VMEM)] * len(arrays)
        specs += [pl.BlockSpec(memory_space=pl.ANY)] * len(after)
        return kernel_call(kernel, outs, specs, name, scratch, flops)(*arrays, *after)

    return run


def shape(dims, kind):
    return jax.ShapeDtypeStruct(dims, kind)


def quotient(value, divisor):
    return jnp.floor((value.astype(F32) + 0.5) * (1.0 / divisor)).astype(jnp.int32)


def as_column(row):
    return jnp.transpose(jnp.broadcast_to(row, (TILE, TILE)))


def slot_parts(send_rows, counts, rows):
    send_rows = jnp.transpose(send_rows.astype(F32)).astype(jnp.int32)
    owners, slots = send_rows.shape
    count = as_column(counts.astype(F32))[:, :slots]
    lane = iota((owners, slots), 1).astype(F32)
    key = jnp.where(lane < count, send_rows, rows)
    high = (key >> 5).astype(F32).astype(BF16)
    low = (key & 31).astype(F32).astype(BF16)
    total = owners * slots
    expand = one_hot(quotient(iota((total, owners), 0), slots) == iota((total, owners), 1))
    row = iota((total, slots), 0)
    mine = row - quotient(row, slots) * slots == iota((total, slots), 1)
    high = jnp.where(mine, dot(expand, high) * 32.0, 0.0).astype(BF16)
    low = jnp.where(mine, dot(expand, low), 0.0).astype(BF16)
    return high, low


def start_kernel(*refs):
    out_ref, degree_ref, bias_ref, table_ref, key_ref = refs[8:13]
    features_ref, rows_ref, counts_ref, *parts, sems = refs[13:]
    pairs = tuple(zip(refs[:8], (features_ref, rows_ref, counts_ref, degree_ref, *parts, bias_ref)))
    copies = [pltpu.make_async_copy(a, b, sems.at[k]) for k, (a, b) in enumerate(pairs)]
    for copy in copies:
        copy.start()
    for copy in copies:
        copy.wait()
    rows = features_ref.shape[0]
    slots = rows_ref.shape[0]
    high, low = slot_parts(rows_ref[...], counts_ref[...], rows)
    ones = jnp.ones((slots, TILE), BF16)
    key = dot(high, ones) + dot(low, ones)
    lane = iota(key.shape, 1).astype(F32)
    pick = jnp.concatenate(
        [one_hot(key == lane + float(start)) for start in range(0, rows, TILE)], axis=1
    )
    sent = dot(pick, features_ref[...])
    out_ref[...] = jnp.where(key >= float(rows), UNUSED, sent).astype(BF16)
    ones = jnp.ones((8, slots), BF16)
    key_ref[...] = dot(ones, high, NT) + dot(ones, low, NT)
    place = 0
    for part in parts:
        table_ref[place : place + part.shape[0]] = part[...]
        place += part.shape[0]
    odd = lax.rem(lax.axis_index("blk"), 2)
    table_ref[place : place + 1] = jnp.full((1, table_ref.shape[1]), odd, jnp.int32)


def start_call(features, send_rows, counts_row, degree, tables, bias_row):
    rows, width = features.shape
    total = send_rows.size
    small = (features, send_rows, counts_row, degree, *tables)
    arrays = [pltpu.with_memory_space_constraint(a, pltpu.HBM) for a in (*small, bias_row)]
    return pl.pallas_call(
        start_kernel,
        out_shape=(
            shape((total, width), BF16),
            shape(degree.shape, F32),
            shape(bias_row.shape, F32),
            shape((1 + sum(a.shape[0] for a in tables), tables[0].shape[1]), jnp.int32),
            shape((8, total), F32),
        ),
        in_specs=[pl.BlockSpec(memory_space=pltpu.HBM)] * 8,
        scratch_shapes=[pltpu.VMEM(a.shape, a.dtype) for a in (features, send_rows, counts_row, *tables)]
        + [pltpu.SemaphoreType.DMA((8,))],
        compiler_params=pltpu.CompilerParams(vmem_limit_bytes=8 * 1024 * 1024),
        cost_estimate=pl.CostEstimate(flops=10**8, bytes_accessed=10**6, transcendentals=0),
        name="start",
    )(*arrays)


def transpose_kernel(tiles_ref, *refs):
    out_ref = refs[-1]
    for t in range(tiles_ref.shape[0]):
        out_ref[t] = jnp.transpose(tiles_ref[t].astype(F32)).astype(BF16)


def used_slots(ref):
    return jnp.where(ref[...].astype(F32) < 512.0, 1.0, 0.0).astype(BF16)


def scaled_rows(degree_ref, values):
    count = values.shape[0] // TILE
    parts = [
        as_column(degree_ref[t : t + 1]) * values[t * TILE : (t + 1) * TILE] for t in range(count)
    ]
    return jnp.concatenate(parts, axis=0)


def place_kernel(incoming_ref, degree_ref, out_ref):
    rows = out_ref.shape[0]
    used = used_slots(incoming_ref)
    before = one_hot(iota((TILE, TILE), 0) < iota((TILE, TILE), 1))
    ones = jnp.ones((TILE, TILE), BF16)
    mean = jnp.full((8, TILE), 1.0 / TILE, BF16)
    offset = jnp.zeros((8, TILE), F32)
    parts = []
    for start in range(0, used.shape[0], TILE):
        here = dot(mean, used[start : start + TILE], NT)
        flags = here.astype(BF16)
        rank = jnp.where(here > 0.5, dot(flags, before) + offset, -1.0)
        offset = offset + dot(flags, ones)
        parts.append(one_hot(iota((rows, TILE), 0).astype(F32) == rank[0:1]))
    owned = dot(jnp.concatenate(parts, axis=1), incoming_ref[...])
    out_ref[...] = scaled_rows(degree_ref, owned).astype(BF16)


def unplace_kernel(incoming_ref, out_ref):
    rows = out_ref.shape[1]
    used = used_slots(incoming_ref)
    before = one_hot(iota((TILE, TILE), 1) < iota((TILE, TILE), 0))
    ones = jnp.ones((TILE, TILE), BF16)
    offset = jnp.zeros((TILE, TILE), F32)
    lane = iota((TILE, TILE), 1).astype(F32)
    for start in range(0, used.shape[0], TILE):
        here = used[start : start + TILE]
        rank = jnp.where(here.astype(F32) > 0.5, dot(before, here) + offset, -1.0)
        offset = offset + dot(ones, here)
        for column in range(0, rows, TILE):
            out_ref[start : start + TILE, column : column + TILE] = one_hot(
                rank == lane + float(column)
            )


def gather_kernel(table_ref, tiles_ref, src0, two, apart, near, *refs):
    out_ref, acc_ref = refs[-2:]
    acc_ref[...] = jnp.zeros_like(acc_ref)
    most = table_ref.shape[1]
    steps = tiles_ref.shape[0] // most
    odd = table_ref[2 * steps + 1, 0]
    for step, source in ((0, src0), (2, two), (3 - 2 * odd, apart), (1 + 2 * odd, near)):
        for k in range(most):
            col = pl.multiple_of(table_ref[steps + step, k] * TILE, TILE)
            row = pl.multiple_of(table_ref[step, k] * TILE, TILE)
            live = (k < table_ref[2 * steps, step]).astype(F32)
            prod = dot(tiles_ref[step * most + k], source[pl.ds(col, TILE), :])
            acc_ref[pl.ds(row, TILE), :] += prod * live
    quarters, rows, _ = out_ref.shape
    for q in range(quarters):
        out_ref[q] = acc_ref[q * rows : (q + 1) * rows].astype(BF16)


def dense_kernel(
    parts_ref, degree_ref, weight_ref, bias_ref, out_grad_ref, hidden_ref, out_ref, agg_ref, grad_pre_ref
):
    quarters, rows, width = parts_ref.shape
    summed = parts_ref[0].astype(F32)
    for q in range(1, quarters):
        summed = summed + parts_ref[q].astype(F32)
    for t in range(rows // TILE):
        part = slice(t * TILE, (t + 1) * TILE)
        scale = as_column(degree_ref[t : t + 1])
        agg = (scale * summed[part]).astype(BF16)
        agg_ref[part] = agg
        pre = dot(agg, weight_ref[...]) + bias_ref[...]
        sig = jax.nn.sigmoid(pre)
        hidden_ref[part] = (pre * sig).astype(BF16)
        grad_pre = (
            out_grad_ref[part].astype(F32) * (sig * (1.0 + pre * (1.0 - sig)))
        ).astype(BF16)
        grad_pre_ref[part] = grad_pre
        grad_agg = (scale * dot(grad_pre, weight_ref[...], NT)).astype(BF16)
        for q in range(quarters):
            out_ref[q, part] = grad_agg
    grad_pre = grad_pre_ref[...]
    term = dot(agg_ref[...], grad_pre, TN).astype(BF16)
    total = jnp.sum(grad_pre.astype(F32), axis=0, keepdims=True)
    high = total.astype(BF16).astype(F32)
    pieces = (high[:, :TILE], high[:, TILE:], (total - high)[:, :TILE], (total - high)[:, TILE:])
    row = iota((16, TILE), 0)
    ends = jnp.zeros((16, TILE), F32)
    for k, piece in enumerate(pieces):
        ends = jnp.where(row == k, piece, ends)
    for q in range(quarters):
        out_ref[q, rows : rows + width] = term[:, :TILE]
        out_ref[q, rows + width : rows + 2 * width] = term[:, TILE:]
        out_ref[q, rows + 2 * width :] = ends.astype(BF16)


def terms_kernel(block_ref, *refs):
    out_ref = refs[-1]
    quarters, all_rows, width = block_ref.shape
    rows = all_rows - 2 * width - 16
    total = block_ref[0, rows:].astype(F32)
    for q in range(1, quarters):
        total = total + block_ref[q, rows:].astype(F32)
    ends = total[2 * width :]
    lines = (4 * width, width)
    out = jnp.zeros((4 * width, TILE), F32)
    for k in range(4):
        if k < 2:
            piece = total[k * width : (k + 1) * width]
        else:
            bias = ends[k - 2 : k - 1] + ends[k : k + 1]
            mine = (iota((width, TILE), 1) + (k - 2) * TILE) // 2 == iota((width, TILE), 0)
            piece = jnp.where(mine, bias, 0.0)
        here = iota(lines, 0) == 4 * iota(lines, 1) + k
        out = out + dot(one_hot(here), piece.astype(BF16))
    out_ref[...] = out.astype(BF16)


def spread_kernel(table_ref, tiles_ref, block_ref, *refs):
    own_ref, two_ref, near_ref, apart_ref, acc_ref = refs[-5:]
    acc_ref[...] = jnp.zeros_like(acc_ref)
    most = table_ref.shape[1]
    steps = tiles_ref.shape[0] // most
    col_tiles = own_ref.shape[0] // TILE
    for step in range(steps - 1, -1, -1):
        for k in range(most):
            col = pl.multiple_of(table_ref[steps + step, k] * TILE, TILE)
            quarter = table_ref[step, k] // col_tiles
            row = pl.multiple_of(table_ref[step, k] % col_tiles * TILE, TILE)
            live = (k < table_ref[2 * steps, step]).astype(F32)
            prod = dot(tiles_ref[step * most + k], block_ref[quarter, pl.ds(row, TILE), :])
            acc_ref[step, pl.ds(col, TILE), :] += prod * live
    odd = table_ref[2 * steps + 1, 0]
    own_ref[...] = acc_ref[0]
    two_ref[...] = acc_ref[2]
    near_ref[...] = acc_ref[1 + 2 * odd].astype(BF16)
    apart_ref[...] = acc_ref[3 - 2 * odd].astype(BF16)


def add_kernel(a_ref, b_ref, out_ref):
    out_ref[...] = (a_ref[...] + b_ref[...].astype(F32)).astype(BF16)


def slot_of(lines, dim):
    index = iota(lines, dim)
    owner = quotient(index, 12)
    return owner, index - 12 * owner


def back_kernel(own_ref, in1, in2, degree_ref, unplace_ref, terms_ref, out_ref):
    total = own_ref[...] + in1[...].astype(F32) + in2[...].astype(F32)
    grads = scaled_rows(degree_ref, total).astype(BF16)
    slots = dot(unplace_ref[...], grads).astype(BF16)
    count, width = terms_ref.shape
    pairs = jnp.sum(terms_ref[...].astype(F32).reshape(count // 8, 8, width), axis=0)
    term = jnp.concatenate([pairs[:4] + pairs[4:], jnp.zeros((TILE - 4, width), F32)], axis=0)
    term = term.astype(BF16)
    lines = (TILE // 8 * 12, TILE)
    owner, slot = slot_of(lines, 0)
    widen = one_hot((slot < 8) & (owner * 8 + slot == iota(lines, 1)))
    ends = dot(one_hot(slot == 8 + iota(lines, 1)), term)
    for t in range(slots.shape[0] // TILE):
        group = dot(widen, slots[t * TILE : (t + 1) * TILE]) + ends
        out_ref[t * lines[0] : (t + 1) * lines[0]] = group.astype(BF16)


def last_kernel(key_ref, returned_ref, out_ref, weight_ref, bias_ref):
    rows = out_ref.shape[0]
    owners = TILE // 8
    lines = (TILE + 3 * owners, 12 * owners)
    owner, slot = slot_of(lines, 1)
    row = iota(lines, 0)
    wanted = (slot < 8) & (owner * 8 + slot == row)
    wanted |= (slot == 8) & (owner + TILE == row)
    wanted |= (slot == 9) & (owner + TILE + owners == row)
    wanted |= ((slot == 10) & (row == TILE + 2 * owners)) | ((slot == 11) & (row == TILE + 2 * owners + 1))
    pick = one_hot(wanted)
    total = jnp.zeros((rows, TILE), F32)
    bias = jnp.zeros((owners, TILE), F32)
    for t in range(returned_ref.shape[0] // lines[1]):
        found = dot(pick, returned_ref[t * lines[1] : (t + 1) * lines[1]])
        span = slice(t * TILE, (t + 1) * TILE)
        here = one_hot(iota((rows, TILE), 0).astype(F32) == key_ref[0:1, span])
        total = total + dot(here, found[:TILE].astype(BF16))
        for k in range(2):
            part = found[TILE + k * owners : TILE + (k + 1) * owners]
            weight_ref[t * owners : (t + 1) * owners, k * TILE : (k + 1) * TILE] = part
        bias = bias + found[TILE + 2 * owners :]
    out_ref[...] = total.astype(BF16)
    bias_ref[:, :TILE] = bias[0:1]
    bias_ref[:, TILE:] = bias[1:2]


def moved(value, target):
    count = lax.axis_size("blk")
    return lax.ppermute(value, "blk", [(s, target(s) % count) for s in range(count)])


def two_on(blk):
    return blk + 2


def two_back(blk):
    return blk - 2


def apart_on(blk):
    return blk + 1 + 2 * (blk % 2)


def apart_back(blk):
    return blk - 3 + 2 * (blk % 2)


def other_core(blk):
    return blk + 1 - 2 * (blk % 2)


def exchange(value, axis):
    return lax.all_to_all(value, axis, split_axis=0, concat_axis=0, tiled=True)


def tile_call(kernel, outs, scratch, name, table, arrays, after=()):
    specs = [pl.BlockSpec(memory_space=pltpu.SMEM)]
    specs += [pl.BlockSpec(memory_space=pltpu.VMEM)] * len(arrays)
    specs += [pl.BlockSpec(memory_space=pl.ANY)] * len(after)
    return kernel_call(kernel, outs, specs, name, scratch)(table, *arrays, *after)


def on_device(
    features,
    send_rows,
    send_counts,
    tile_values,
    tile_rows,
    tile_cols,
    tile_counts,
    degree_scale,
    weight,
    bias,
    out_grad,
):
    blocks = lax.axis_size("blk")
    quarters = lax.axis_size("rep")
    rows, width = features.shape
    slots = send_rows.shape[1]
    steps, most = tile_values.shape[:2]
    hidden_width = weight.shape[1]
    total = blocks * slots
    slot_rows = send_rows.T
    counts_row = send_counts.reshape(1, blocks)
    degree = degree_scale.reshape(rows // TILE, TILE)
    tiles = tile_values.reshape(steps * most, TILE, TILE)
    tables = (tile_rows, tile_cols, tile_counts.reshape(1, steps))

    outgoing, scale, bias_row, table, key = start_call(
        features, slot_rows, counts_row, degree, tables, bias.reshape(1, hidden_width)
    )
    incoming = exchange(outgoing.reshape(blocks, slots, width), "blk").reshape(total, width)
    scaled = call(place_kernel, shape((rows, width), BF16), "place")(incoming, scale)
    two = moved(scaled, two_on)
    sources = (scaled, two, moved(scaled, apart_on), moved(two, other_core))
    unplace = call(unplace_kernel, shape((total, rows), BF16), "unplace", flops=10**8)(incoming)
    turned = call(transpose_kernel, shape(tiles.shape, BF16), "turn", flops=LONG)(
        tiles, after=(scaled,)
    )
    partial = tile_call(
        gather_kernel,
        shape((quarters, rows, width), BF16),
        [pltpu.VMEM((quarters * rows, width), F32)],
        "gather_tiles",
        table,
        (tiles, *sources),
        (turned, unplace),
    )
    parts = exchange(partial, "rep")
    hidden, sent = call(
        dense_kernel,
        (
            shape((rows, hidden_width), BF16),
            shape((quarters, rows + 2 * width + 16, width), BF16),
        ),
        "dense",
        (pltpu.VMEM((rows, width), BF16), pltpu.VMEM((rows, hidden_width), BF16)),
    )(parts, scale, weight, bias_row, out_grad)
    block = exchange(sent, "rep")
    terms = call(terms_kernel, shape((4 * width, TILE), BF16), "terms")(block)
    lines = terms
    terms = exchange(terms.reshape(blocks, 4, TILE), "blk").reshape(4 * width, TILE)

    own, two, near, apart = tile_call(
        spread_kernel,
        (shape((rows, width), F32),) * 2 + (shape((rows, width), BF16),) * 2,
        [pltpu.VMEM((steps, rows, width), F32)],
        "spread_tiles",
        table,
        (turned, block),
        (lines,),
    )
    near = moved(near, other_core)
    apart = moved(apart, apart_back)
    two = moved(call(add_kernel, shape((rows, width), BF16), "add")(two, near), two_back)
    back = call(back_kernel, shape((blocks * (slots + 4), width), BF16), "back")(
        own, apart, two, scale, unplace, terms
    )
    returned = exchange(back.reshape(blocks, 3, 4, width), "blk").reshape(back.shape)
    grad_features, grad_weight, grad_bias = call(
        last_kernel,
        (shape((rows, width), BF16), shape(weight.shape, F32), shape((1, hidden_width), F32)),
        "last",
    )(key, returned)
    return (hidden, grad_features, grad_weight, grad_bias.reshape(hidden_width))


def solution(mesh):
    in_specs = (
        P(("blk", "rep"), None),
        P(("blk", "rep"), None),
        P(("blk", "rep")),
        P(("blk", "rep"), None, None, None),
        P(("blk", "rep"), None),
        P(("blk", "rep"), None),
        P(("blk", "rep")),
        P(("blk", "rep")),
        P(),
        P(),
        P(("blk", "rep"), None),
    )
    out_specs = (P(("blk", "rep"), None), P(("blk", "rep"), None), P(), P())
    return jax.shard_map(
        on_device, mesh=mesh, in_specs=in_specs, out_specs=out_specs, check_vma=False
    )
```

```python
import jax
import jax.numpy as jnp
from jax import lax
from jax.experimental import pallas as pl
from jax.experimental.pallas import tpu as pltpu
from jax.sharding import PartitionSpec as P

BF16 = jnp.bfloat16
F32 = jnp.float32
TILE = 128
LONG = 10**11
UNUSED = 1024.0
NN = (((1,), (0,)), ((), ()))
NT = (((1,), (1,)), ((), ()))
TN = (((0,), (0,)), ((), ()))


def dot(a, b, dims=NN):
    return lax.dot_general(a, b, dims, preferred_element_type=F32)


def iota(shape, dim):
    return lax.broadcasted_iota(jnp.int32, shape, dim)


def one_hot(mask):
    return jnp.where(mask, 1.0, 0.0).astype(BF16)


def kernel_call(kernel, outs, specs, name, scratch=(), flops=10**8):
    return pl.pallas_call(
        kernel,
        out_shape=outs,
        in_specs=specs,
        scratch_shapes=list(scratch),
        compiler_params=pltpu.CompilerParams(vmem_limit_bytes=16 * 1024 * 1024),
        cost_estimate=pl.CostEstimate(flops=flops, bytes_accessed=10**6, transcendentals=0),
        name=name,
    )


def call(kernel, outs, name, scratch=(), flops=10**8):
    def run(*arrays, after=()):
        specs = [pl.BlockSpec(memory_space=pltpu.VMEM)] * len(arrays)
        specs += [pl.BlockSpec(memory_space=pl.ANY)] * len(after)
        return kernel_call(kernel, outs, specs, name, scratch, flops)(*arrays, *after)

    return run


def shape(dims, kind):
    return jax.ShapeDtypeStruct(dims, kind)


def quotient(value, divisor):
    return jnp.floor((value.astype(F32) + 0.5) * (1.0 / divisor)).astype(jnp.int32)


def as_column(row):
    return jnp.transpose(jnp.broadcast_to(row, (TILE, TILE)))


def slot_parts(send_rows, counts, rows):
    send_rows = jnp.transpose(send_rows.astype(F32)).astype(jnp.int32)
    owners, slots = send_rows.shape
    count = as_column(counts.astype(F32))[:, :slots]
    lane = iota((owners, slots), 1).astype(F32)
    key = jnp.where(lane < count, send_rows, rows)
    high = (key >> 5).astype(F32).astype(BF16)
    low = (key & 31).astype(F32).astype(BF16)
    total = owners * slots
    expand = one_hot(quotient(iota((total, owners), 0), slots) == iota((total, owners), 1))
    row = iota((total, slots), 0)
    mine = row - quotient(row, slots) * slots == iota((total, slots), 1)
    high = jnp.where(mine, dot(expand, high) * 32.0, 0.0).astype(BF16)
    low = jnp.where(mine, dot(expand, low), 0.0).astype(BF16)
    return high, low


def start_kernel(*refs):
    out_ref, degree_ref, bias_ref, table_ref, key_ref = refs[8:13]
    features_ref, rows_ref, counts_ref, *parts, sems = refs[13:]
    pairs = tuple(zip(refs[:8], (features_ref, rows_ref, counts_ref, degree_ref, *parts, bias_ref)))
    copies = [pltpu.make_async_copy(a, b, sems.at[k]) for k, (a, b) in enumerate(pairs)]
    for copy in copies:
        copy.start()
    for copy in copies:
        copy.wait()
    rows = features_ref.shape[0]
    slots = rows_ref.shape[0]
    high, low = slot_parts(rows_ref[...], counts_ref[...], rows)
    ones = jnp.ones((slots, TILE), BF16)
    key = dot(high, ones) + dot(low, ones)
    lane = iota(key.shape, 1).astype(F32)
    pick = jnp.concatenate(
        [one_hot(key == lane + float(start)) for start in range(0, rows, TILE)], axis=1
    )
    sent = dot(pick, features_ref[...])
    out_ref[...] = jnp.where(key >= float(rows), UNUSED, sent).astype(BF16)
    ones = jnp.ones((8, slots), BF16)
    key_ref[...] = dot(ones, high, NT) + dot(ones, low, NT)
    place = 0
    for part in parts:
        table_ref[place : place + part.shape[0]] = part[...]
        place += part.shape[0]
    odd = lax.rem(lax.axis_index("blk"), 2)
    table_ref[place : place + 1] = jnp.full((1, table_ref.shape[1]), odd, jnp.int32)


def start_call(features, send_rows, counts_row, degree, tables, bias_row):
    rows, width = features.shape
    total = send_rows.size
    small = (features, send_rows, counts_row, degree, *tables)
    arrays = [pltpu.with_memory_space_constraint(a, pltpu.HBM) for a in (*small, bias_row)]
    return pl.pallas_call(
        start_kernel,
        out_shape=(
            shape((total, width), BF16),
            shape(degree.shape, F32),
            shape(bias_row.shape, F32),
            shape((1 + sum(a.shape[0] for a in tables), tables[0].shape[1]), jnp.int32),
            shape((8, total), F32),
        ),
        in_specs=[pl.BlockSpec(memory_space=pltpu.HBM)] * 8,
        scratch_shapes=[pltpu.VMEM(a.shape, a.dtype) for a in (features, send_rows, counts_row, *tables)]
        + [pltpu.SemaphoreType.DMA((8,))],
        compiler_params=pltpu.CompilerParams(vmem_limit_bytes=8 * 1024 * 1024),
        cost_estimate=pl.CostEstimate(flops=10**8, bytes_accessed=10**6, transcendentals=0),
        name="start",
    )(*arrays)


def transpose_kernel(tiles_ref, *refs):
    out_ref = refs[-1]
    for t in range(tiles_ref.shape[0]):
        out_ref[t] = jnp.transpose(tiles_ref[t].astype(F32)).astype(BF16)


def used_slots(ref):
    return jnp.where(ref[...].astype(F32) < 512.0, 1.0, 0.0).astype(BF16)


def scaled_rows(degree_ref, values):
    count = values.shape[0] // TILE
    parts = [
        as_column(degree_ref[t : t + 1]) * values[t * TILE : (t + 1) * TILE] for t in range(count)
    ]
    return jnp.concatenate(parts, axis=0)


def place_kernel(incoming_ref, degree_ref, out_ref):
    rows = out_ref.shape[0]
    used = used_slots(incoming_ref)
    before = one_hot(iota((TILE, TILE), 0) < iota((TILE, TILE), 1))
    ones = jnp.ones((TILE, TILE), BF16)
    mean = jnp.full((8, TILE), 1.0 / TILE, BF16)
    offset = jnp.zeros((8, TILE), F32)
    parts = []
    for start in range(0, used.shape[0], TILE):
        here = dot(mean, used[start : start + TILE], NT)
        flags = here.astype(BF16)
        rank = jnp.where(here > 0.5, dot(flags, before) + offset, -1.0)
        offset = offset + dot(flags, ones)
        parts.append(one_hot(iota((rows, TILE), 0).astype(F32) == rank[0:1]))
    owned = dot(jnp.concatenate(parts, axis=1), incoming_ref[...])
    out_ref[...] = scaled_rows(degree_ref, owned).astype(BF16)


def unplace_kernel(incoming_ref, out_ref):
    rows = out_ref.shape[1]
    used = used_slots(incoming_ref)
    before = one_hot(iota((TILE, TILE), 1) < iota((TILE, TILE), 0))
    ones = jnp.ones((TILE, TILE), BF16)
    offset = jnp.zeros((TILE, TILE), F32)
    lane = iota((TILE, TILE), 1).astype(F32)
    for start in range(0, used.shape[0], TILE):
        here = used[start : start + TILE]
        rank = jnp.where(here.astype(F32) > 0.5, dot(before, here) + offset, -1.0)
        offset = offset + dot(ones, here)
        for column in range(0, rows, TILE):
            out_ref[start : start + TILE, column : column + TILE] = one_hot(
                rank == lane + float(column)
            )


def gather_kernel(table_ref, tiles_ref, src0, two, apart, near, *refs):
    out_ref, acc_ref = refs[-2:]
    acc_ref[...] = jnp.zeros_like(acc_ref)
    most = table_ref.shape[1]
    steps = tiles_ref.shape[0] // most
    odd = table_ref[2 * steps + 1, 0]
    for step, source in ((0, src0), (2, two), (3 - 2 * odd, apart), (1 + 2 * odd, near)):
        for k in range(most):
            col = pl.multiple_of(table_ref[steps + step, k] * TILE, TILE)
            row = pl.multiple_of(table_ref[step, k] * TILE, TILE)
            live = (k < table_ref[2 * steps, step]).astype(F32)
            prod = dot(tiles_ref[step * most + k], source[pl.ds(col, TILE), :])
            acc_ref[pl.ds(row, TILE), :] += prod * live
    quarters, rows, _ = out_ref.shape
    for q in range(quarters):
        out_ref[q] = acc_ref[q * rows : (q + 1) * rows].astype(BF16)


def dense_kernel(
    parts_ref, degree_ref, weight_ref, bias_ref, out_grad_ref, hidden_ref, out_ref, agg_ref, grad_pre_ref
):
    quarters, rows, width = parts_ref.shape
    summed = parts_ref[0].astype(F32)
    for q in range(1, quarters):
        summed = summed + parts_ref[q].astype(F32)
    for t in range(rows // TILE):
        part = slice(t * TILE, (t + 1) * TILE)
        scale = as_column(degree_ref[t : t + 1])
        agg = (scale * summed[part]).astype(BF16)
        agg_ref[part] = agg
        pre = dot(agg, weight_ref[...]) + bias_ref[...]
        sig = jax.nn.sigmoid(pre)
        hidden_ref[part] = (pre * sig).astype(BF16)
        grad_pre = (
            out_grad_ref[part].astype(F32) * (sig * (1.0 + pre * (1.0 - sig)))
        ).astype(BF16)
        grad_pre_ref[part] = grad_pre
        grad_agg = (scale * dot(grad_pre, weight_ref[...], NT)).astype(BF16)
        for q in range(quarters):
            out_ref[q, part] = grad_agg
    grad_pre = grad_pre_ref[...]
    term = dot(agg_ref[...], grad_pre, TN).astype(BF16)
    total = jnp.sum(grad_pre.astype(F32), axis=0, keepdims=True)
    high = total.astype(BF16).astype(F32)
    pieces = (high[:, :TILE], high[:, TILE:], (total - high)[:, :TILE], (total - high)[:, TILE:])
    row = iota((16, TILE), 0)
    ends = jnp.zeros((16, TILE), F32)
    for k, piece in enumerate(pieces):
        ends = jnp.where(row == k, piece, ends)
    for q in range(quarters):
        out_ref[q, rows : rows + width] = term[:, :TILE]
        out_ref[q, rows + width : rows + 2 * width] = term[:, TILE:]
        out_ref[q, rows + 2 * width :] = ends.astype(BF16)


def terms_halves(block_ref):
    quarters, all_rows, width = block_ref.shape
    rows = all_rows - 2 * width - 16
    total = block_ref[0, rows:].astype(F32)
    for q in range(1, quarters):
        total = total + block_ref[q, rows:].astype(F32)
    ends = total[2 * width :]
    half = width // 2
    lines = (4 * half, half)
    out = [jnp.zeros((4 * half, TILE), F32) for _ in range(2)]
    for k in range(4):
        if k < 2:
            piece = total[k * width : (k + 1) * width]
        else:
            bias = ends[k - 2 : k - 1] + ends[k : k + 1]
            mine = (iota((width, TILE), 1) + (k - 2) * TILE) // 2 == iota((width, TILE), 0)
            piece = jnp.where(mine, bias, 0.0)
        here = one_hot(iota(lines, 0) == 4 * iota(lines, 1) + k)
        piece = piece.astype(BF16)
        out = [out[h] + dot(here, piece[h * half : (h + 1) * half]) for h in range(2)]
    return out


def spread_kernel(table_ref, tiles_ref, block_ref, *refs):
    own_ref, two_ref, near_ref, apart_ref, mine_ref, acc_ref = refs
    acc_ref[...] = jnp.zeros_like(acc_ref)
    most = table_ref.shape[1]
    steps = tiles_ref.shape[0] // most
    col_tiles = own_ref.shape[0] // TILE
    for step in range(steps - 1, -1, -1):
        for k in range(most):
            col = pl.multiple_of(table_ref[steps + step, k] * TILE, TILE)
            quarter = table_ref[step, k] // col_tiles
            row = pl.multiple_of(table_ref[step, k] % col_tiles * TILE, TILE)
            live = (k < table_ref[2 * steps, step]).astype(F32)
            prod = dot(tiles_ref[step * most + k], block_ref[quarter, pl.ds(row, TILE), :])
            acc_ref[step, pl.ds(col, TILE), :] += prod * live
    odd = table_ref[2 * steps + 1, 0]
    own_ref[...] = acc_ref[0]
    two_ref[...] = acc_ref[2]
    rows = own_ref.shape[0]
    near_ref[:rows] = acc_ref[1 + 2 * odd].astype(BF16)
    first, second = terms_halves(block_ref)
    mine_ref[...] = jnp.where(odd == 0, first, second)
    near_ref[rows:] = jnp.where(odd == 0, second, first).astype(BF16)
    apart_ref[...] = acc_ref[3 - 2 * odd].astype(BF16)


def add_kernel(two_ref, mine_ref, near_ref, out_ref, terms_ref):
    rows = out_ref.shape[0]
    out_ref[...] = (two_ref[...] + near_ref[:rows].astype(F32)).astype(BF16)
    terms_ref[...] = (mine_ref[...] + near_ref[rows:].astype(F32)).astype(BF16)


def slot_of(lines, dim):
    index = iota(lines, dim)
    owner = quotient(index, 12)
    return owner, index - 12 * owner


def back_kernel(own_ref, in1, in2, degree_ref, unplace_ref, terms_ref, out_ref):
    total = own_ref[...] + in1[...].astype(F32) + in2[...].astype(F32)
    grads = scaled_rows(degree_ref, total).astype(BF16)
    slots = dot(unplace_ref[...], grads).astype(BF16)
    count, width = terms_ref.shape
    pairs = jnp.sum(terms_ref[...].astype(F32).reshape(count // 8, 8, width), axis=0)
    term = jnp.concatenate([pairs[:4] + pairs[4:], jnp.zeros((TILE - 4, width), F32)], axis=0)
    term = term.astype(BF16)
    lines = (TILE // 8 * 12, TILE)
    owner, slot = slot_of(lines, 0)
    widen = one_hot((slot < 8) & (owner * 8 + slot == iota(lines, 1)))
    ends = dot(one_hot(slot == 8 + iota(lines, 1)), term)
    for t in range(slots.shape[0] // TILE):
        group = dot(widen, slots[t * TILE : (t + 1) * TILE]) + ends
        out_ref[t * lines[0] : (t + 1) * lines[0]] = group.astype(BF16)


def last_kernel(key_ref, returned_ref, out_ref, weight_ref, bias_ref):
    rows = out_ref.shape[0]
    owners = TILE // 8
    lines = (TILE + 3 * owners, 12 * owners)
    owner, slot = slot_of(lines, 1)
    row = iota(lines, 0)
    wanted = (slot < 8) & (owner * 8 + slot == row)
    place = TILE + owner % 2 * (owners // 2) + owner // 2
    wanted |= ((slot == 8) & (place == row)) | ((slot == 9) & (place + owners == row))
    wanted |= ((slot == 10) & (row == TILE + 2 * owners)) | ((slot == 11) & (row == TILE + 2 * owners + 1))
    pick = one_hot(wanted)
    total = jnp.zeros((rows, TILE), F32)
    bias = jnp.zeros((owners, TILE), F32)
    for t in range(returned_ref.shape[0] // lines[1]):
        found = dot(pick, returned_ref[t * lines[1] : (t + 1) * lines[1]])
        span = slice(t * TILE, (t + 1) * TILE)
        here = one_hot(iota((rows, TILE), 0).astype(F32) == key_ref[0:1, span])
        total = total + dot(here, found[:TILE].astype(BF16))
        for k in range(2):
            for core in range(2):
                start = TILE + (2 * k + core) * (owners // 2)
                line = core * (weight_ref.shape[0] // 2) + t * (owners // 2)
                part = found[start : start + owners // 2]
                weight_ref[line : line + owners // 2, k * TILE : (k + 1) * TILE] = part
        bias = bias + found[TILE + 2 * owners :]
    out_ref[...] = total.astype(BF16)
    bias_ref[:, :TILE] = bias[0:1]
    bias_ref[:, TILE:] = bias[1:2]


def moved(value, target):
    count = lax.axis_size("blk")
    return lax.ppermute(value, "blk", [(s, target(s) % count) for s in range(count)])


def two_on(blk):
    return blk + 2


def two_back(blk):
    return blk - 2


def apart_on(blk):
    return blk + 1 + 2 * (blk % 2)


def apart_back(blk):
    return blk - 3 + 2 * (blk % 2)


def other_core(blk):
    return blk + 1 - 2 * (blk % 2)


def exchange(value, axis, groups=None):
    return lax.all_to_all(
        value, axis, split_axis=0, concat_axis=0, axis_index_groups=groups, tiled=True
    )


def tile_call(kernel, outs, scratch, name, table, arrays, after=()):
    specs = [pl.BlockSpec(memory_space=pltpu.SMEM)]
    specs += [pl.BlockSpec(memory_space=pltpu.VMEM)] * len(arrays)
    specs += [pl.BlockSpec(memory_space=pl.ANY)] * len(after)
    return kernel_call(kernel, outs, specs, name, scratch)(table, *arrays, *after)


def on_device(
    features,
    send_rows,
    send_counts,
    tile_values,
    tile_rows,
    tile_cols,
    tile_counts,
    degree_scale,
    weight,
    bias,
    out_grad,
):
    blocks = lax.axis_size("blk")
    quarters = lax.axis_size("rep")
    rows, width = features.shape
    slots = send_rows.shape[1]
    steps, most = tile_values.shape[:2]
    hidden_width = weight.shape[1]
    total = blocks * slots
    slot_rows = send_rows.T
    counts_row = send_counts.reshape(1, blocks)
    degree = degree_scale.reshape(rows // TILE, TILE)
    tiles = tile_values.reshape(steps * most, TILE, TILE)
    tables = (tile_rows, tile_cols, tile_counts.reshape(1, steps))

    outgoing, scale, bias_row, table, key = start_call(
        features, slot_rows, counts_row, degree, tables, bias.reshape(1, hidden_width)
    )
    incoming = exchange(outgoing.reshape(blocks, slots, width), "blk").reshape(total, width)
    scaled = call(place_kernel, shape((rows, width), BF16), "place")(incoming, scale)
    two = moved(scaled, two_on)
    sources = (scaled, two, moved(scaled, apart_on), moved(two, other_core))
    unplace = call(unplace_kernel, shape((total, rows), BF16), "unplace", flops=10**8)(incoming)
    turned = call(transpose_kernel, shape(tiles.shape, BF16), "turn", flops=LONG)(
        tiles, after=(scaled,)
    )
    partial = tile_call(
        gather_kernel,
        shape((quarters, rows, width), BF16),
        [pltpu.VMEM((quarters * rows, width), F32)],
        "gather_tiles",
        table,
        (tiles, *sources),
        (turned, unplace),
    )
    parts = exchange(partial, "rep")
    hidden, sent = call(
        dense_kernel,
        (
            shape((rows, hidden_width), BF16),
            shape((quarters, rows + 2 * width + 16, width), BF16),
        ),
        "dense",
        (pltpu.VMEM((rows, width), BF16), pltpu.VMEM((rows, hidden_width), BF16)),
    )(parts, scale, weight, bias_row, out_grad)
    block = exchange(sent, "rep")
    own, two, near, apart, mine = tile_call(
        spread_kernel,
        (
            shape((rows, width), F32),
            shape((rows, width), F32),
            shape((rows + 2 * width, width), BF16),
            shape((rows, width), BF16),
            shape((2 * width, width), F32),
        ),
        [pltpu.VMEM((steps, rows, width), F32)],
        "spread_tiles",
        table,
        (turned, block),
    )
    near = moved(near, other_core)
    apart = moved(apart, apart_back)
    two, terms = call(
        add_kernel, (shape((rows, width), BF16), shape((2 * width, width), BF16)), "add"
    )(two, mine, near)
    two = moved(two, two_back)
    cores = [list(range(core, blocks, 2)) for core in range(2)]
    terms = exchange(terms.reshape(blocks // 2, 4, width), "blk", cores).reshape(terms.shape)
    back = call(back_kernel, shape((blocks * (slots + 4), width), BF16), "back")(
        own, apart, two, scale, unplace, terms
    )
    returned = exchange(back.reshape(blocks, 3, 4, width), "blk").reshape(back.shape)
    grad_features, grad_weight, grad_bias = call(
        last_kernel,
        (shape((rows, width), BF16), shape(weight.shape, F32), shape((1, hidden_width), F32)),
        "last",
    )(key, returned)
    return (hidden, grad_features, grad_weight, grad_bias.reshape(hidden_width))


def solution(mesh):
    in_specs = (
        P(("blk", "rep"), None),
        P(("blk", "rep"), None),
        P(("blk", "rep")),
        P(("blk", "rep"), None, None, None),
        P(("blk", "rep"), None),
        P(("blk", "rep"), None),
        P(("blk", "rep")),
        P(("blk", "rep")),
        P(),
        P(),
        P(("blk", "rep"), None),
    )
    out_specs = (P(("blk", "rep"), None), P(("blk", "rep"), None), P(), P())
    return jax.shard_map(
        on_device, mesh=mesh, in_specs=in_specs, out_specs=out_specs, check_vma=False
    )
```

```python
import jax
import jax.numpy as jnp
from jax import lax
from jax.experimental import pallas as pl
from jax.experimental.pallas import tpu as pltpu
from jax.sharding import PartitionSpec as P

BF16 = jnp.bfloat16
F32 = jnp.float32
TILE = 128
LONG = 10**11
UNUSED = 1024.0
NN = (((1,), (0,)), ((), ()))
NT = (((1,), (1,)), ((), ()))
TN = (((0,), (0,)), ((), ()))


def dot(a, b, dims=NN):
    return lax.dot_general(a, b, dims, preferred_element_type=F32)


def iota(shape, dim):
    return lax.broadcasted_iota(jnp.int32, shape, dim)


def one_hot(mask):
    return jnp.where(mask, 1.0, 0.0).astype(BF16)


def kernel_call(kernel, outs, specs, name, scratch=(), flops=10**8):
    return pl.pallas_call(
        kernel,
        out_shape=outs,
        in_specs=specs,
        scratch_shapes=list(scratch),
        compiler_params=pltpu.CompilerParams(vmem_limit_bytes=16 * 1024 * 1024),
        cost_estimate=pl.CostEstimate(flops=flops, bytes_accessed=10**6, transcendentals=0),
        name=name,
    )


def call(kernel, outs, name, scratch=(), flops=10**8):
    def run(*arrays, after=()):
        specs = [pl.BlockSpec(memory_space=pltpu.VMEM)] * len(arrays)
        specs += [pl.BlockSpec(memory_space=pl.ANY)] * len(after)
        return kernel_call(kernel, outs, specs, name, scratch, flops)(*arrays, *after)

    return run


def shape(dims, kind):
    return jax.ShapeDtypeStruct(dims, kind)


def quotient(value, divisor):
    return jnp.floor((value.astype(F32) + 0.5) * (1.0 / divisor)).astype(jnp.int32)


def as_column(row):
    return jnp.transpose(jnp.broadcast_to(row, (TILE, TILE)))


def slot_parts(send_rows, counts, rows):
    send_rows = jnp.transpose(send_rows.astype(F32)).astype(jnp.int32)
    owners, slots = send_rows.shape
    count = as_column(counts.astype(F32))[:, :slots]
    lane = iota((owners, slots), 1).astype(F32)
    key = jnp.where(lane < count, send_rows, rows)
    high = (key >> 5).astype(F32).astype(BF16)
    low = (key & 31).astype(F32).astype(BF16)
    total = owners * slots
    expand = one_hot(quotient(iota((total, owners), 0), slots) == iota((total, owners), 1))
    row = iota((total, slots), 0)
    mine = row - quotient(row, slots) * slots == iota((total, slots), 1)
    high = jnp.where(mine, dot(expand, high) * 32.0, 0.0).astype(BF16)
    low = jnp.where(mine, dot(expand, low), 0.0).astype(BF16)
    return high, low


def start_kernel(*refs):
    out_ref, degree_ref, bias_ref, table_ref, key_ref = refs[8:13]
    features_ref, rows_ref, counts_ref, *parts, sems = refs[13:]
    pairs = tuple(zip(refs[:8], (features_ref, rows_ref, counts_ref, degree_ref, *parts, bias_ref)))
    copies = [pltpu.make_async_copy(a, b, sems.at[k]) for k, (a, b) in enumerate(pairs)]
    for copy in copies:
        copy.start()
    for copy in copies:
        copy.wait()
    rows = features_ref.shape[0]
    slots = rows_ref.shape[0]
    high, low = slot_parts(rows_ref[...], counts_ref[...], rows)
    ones = jnp.ones((slots, TILE), BF16)
    key = dot(high, ones) + dot(low, ones)
    lane = iota(key.shape, 1).astype(F32)
    pick = jnp.concatenate(
        [one_hot(key == lane + float(start)) for start in range(0, rows, TILE)], axis=1
    )
    sent = dot(pick, features_ref[...])
    out_ref[...] = jnp.where(key >= float(rows), UNUSED, sent).astype(BF16)
    ones = jnp.ones((8, slots), BF16)
    key_ref[...] = dot(ones, high, NT) + dot(ones, low, NT)
    place = 0
    for part in parts:
        table_ref[place : place + part.shape[0]] = part[...]
        place += part.shape[0]
    odd = lax.rem(lax.axis_index("blk"), 2)
    table_ref[place : place + 1] = jnp.full((1, table_ref.shape[1]), odd, jnp.int32)


def start_call(features, send_rows, counts_row, degree, tables, bias_row):
    rows, width = features.shape
    total = send_rows.size
    small = (features, send_rows, counts_row, degree, *tables)
    arrays = [pltpu.with_memory_space_constraint(a, pltpu.HBM) for a in (*small, bias_row)]
    return pl.pallas_call(
        start_kernel,
        out_shape=(
            shape((total, width), BF16),
            shape(degree.shape, F32),
            shape(bias_row.shape, F32),
            shape((1 + sum(a.shape[0] for a in tables), tables[0].shape[1]), jnp.int32),
            shape((8, total), F32),
        ),
        in_specs=[pl.BlockSpec(memory_space=pltpu.HBM)] * 8,
        scratch_shapes=[pltpu.VMEM(a.shape, a.dtype) for a in (features, send_rows, counts_row, *tables)]
        + [pltpu.SemaphoreType.DMA((8,))],
        compiler_params=pltpu.CompilerParams(vmem_limit_bytes=8 * 1024 * 1024),
        cost_estimate=pl.CostEstimate(flops=10**8, bytes_accessed=10**6, transcendentals=0),
        name="start",
    )(*arrays)


def transpose_kernel(tiles_ref, *refs):
    out_ref = refs[-1]
    for t in range(tiles_ref.shape[0]):
        out_ref[t] = jnp.transpose(tiles_ref[t].astype(F32)).astype(BF16)


def used_slots(ref):
    return jnp.where(ref[...].astype(F32) < 512.0, 1.0, 0.0).astype(BF16)


def scaled_rows(degree_ref, values):
    count = values.shape[0] // TILE
    parts = [
        as_column(degree_ref[t : t + 1]) * values[t * TILE : (t + 1) * TILE] for t in range(count)
    ]
    return jnp.concatenate(parts, axis=0)


def place_kernel(incoming_ref, degree_ref, out_ref):
    rows = out_ref.shape[0]
    used = used_slots(incoming_ref)
    before = one_hot(iota((TILE, TILE), 0) < iota((TILE, TILE), 1))
    ones = jnp.ones((TILE, TILE), BF16)
    mean = jnp.full((8, TILE), 1.0 / TILE, BF16)
    offset = jnp.zeros((8, TILE), F32)
    parts = []
    for start in range(0, used.shape[0], TILE):
        here = dot(mean, used[start : start + TILE], NT)
        flags = here.astype(BF16)
        rank = jnp.where(here > 0.5, dot(flags, before) + offset, -1.0)
        offset = offset + dot(flags, ones)
        parts.append(one_hot(iota((rows, TILE), 0).astype(F32) == rank[0:1]))
    owned = dot(jnp.concatenate(parts, axis=1), incoming_ref[...])
    out_ref[...] = scaled_rows(degree_ref, owned).astype(BF16)


def unplace_kernel(incoming_ref, out_ref):
    rows = out_ref.shape[1]
    used = used_slots(incoming_ref)
    before = one_hot(iota((TILE, TILE), 1) < iota((TILE, TILE), 0))
    ones = jnp.ones((TILE, TILE), BF16)
    offset = jnp.zeros((TILE, TILE), F32)
    lane = iota((TILE, TILE), 1).astype(F32)
    for start in range(0, used.shape[0], TILE):
        here = used[start : start + TILE]
        rank = jnp.where(here.astype(F32) > 0.5, dot(before, here) + offset, -1.0)
        offset = offset + dot(ones, here)
        for column in range(0, rows, TILE):
            out_ref[start : start + TILE, column : column + TILE] = one_hot(
                rank == lane + float(column)
            )


def gather_kernel(table_ref, tiles_ref, src0, two, apart, near, *refs):
    out_ref, acc_ref = refs[-2:]
    acc_ref[...] = jnp.zeros_like(acc_ref)
    most = table_ref.shape[1]
    steps = tiles_ref.shape[0] // most
    odd = table_ref[2 * steps + 1, 0]
    for step, source in ((0, src0), (2, two), (3 - 2 * odd, apart), (1 + 2 * odd, near)):
        for k in range(most):
            col = pl.multiple_of(table_ref[steps + step, k] * TILE, TILE)
            row = pl.multiple_of(table_ref[step, k] * TILE, TILE)
            live = (k < table_ref[2 * steps, step]).astype(F32)
            prod = dot(tiles_ref[step * most + k], source[pl.ds(col, TILE), :])
            acc_ref[pl.ds(row, TILE), :] += prod * live
    quarters, rows, _ = out_ref.shape
    for q in range(quarters):
        out_ref[q] = acc_ref[q * rows : (q + 1) * rows].astype(BF16)


def dense_kernel(
    parts_ref, degree_ref, weight_ref, bias_ref, out_grad_ref, hidden_ref, out_ref, agg_ref, grad_pre_ref
):
    quarters, rows, width = parts_ref.shape
    summed = parts_ref[0].astype(F32)
    for q in range(1, quarters):
        summed = summed + parts_ref[q].astype(F32)
    for t in range(rows // TILE):
        part = slice(t * TILE, (t + 1) * TILE)
        scale = as_column(degree_ref[t : t + 1])
        agg = (scale * summed[part]).astype(BF16)
        agg_ref[part] = agg
        pre = dot(agg, weight_ref[...]) + bias_ref[...]
        sig = jax.nn.sigmoid(pre)
        hidden_ref[part] = (pre * sig).astype(BF16)
        grad_pre = (
            out_grad_ref[part].astype(F32) * (sig * (1.0 + pre * (1.0 - sig)))
        ).astype(BF16)
        grad_pre_ref[part] = grad_pre
        grad_agg = (scale * dot(grad_pre, weight_ref[...], NT)).astype(BF16)
        for q in range(quarters):
            out_ref[q, part] = grad_agg
    grad_pre = grad_pre_ref[...]
    term = dot(agg_ref[...], grad_pre, TN).astype(BF16)
    total = jnp.sum(grad_pre.astype(F32), axis=0, keepdims=True)
    high = total.astype(BF16).astype(F32)
    pieces = (high[:, :TILE], high[:, TILE:], (total - high)[:, :TILE], (total - high)[:, TILE:])
    row = iota((16, TILE), 0)
    ends = jnp.zeros((16, TILE), F32)
    for k, piece in enumerate(pieces):
        ends = jnp.where(row == k, piece, ends)
    for q in range(quarters):
        out_ref[q, rows : rows + width] = term[:, :TILE]
        out_ref[q, rows + width : rows + 2 * width] = term[:, TILE:]
        out_ref[q, rows + 2 * width :] = ends.astype(BF16)


def terms_kernel(block_ref, *refs):
    out_ref = refs[-1]
    quarters, all_rows, width = block_ref.shape
    rows = all_rows - 2 * width - 16
    total = block_ref[0, rows:].astype(F32)
    for q in range(1, quarters):
        total = total + block_ref[q, rows:].astype(F32)
    ends = total[2 * width :]
    lines = (4 * width, width)
    out = jnp.zeros((4 * width, TILE), F32)
    for k in range(4):
        if k < 2:
            piece = total[k * width : (k + 1) * width]
        else:
            bias = ends[k - 2 : k - 1] + ends[k : k + 1]
            mine = (iota((width, TILE), 1) + (k - 2) * TILE) // 2 == iota((width, TILE), 0)
            piece = jnp.where(mine, bias, 0.0)
        here = iota(lines, 0) == 4 * iota(lines, 1) + k
        out = out + dot(one_hot(here), piece.astype(BF16))
    out_ref[...] = out.astype(BF16)


def spread_kernel(table_ref, tiles_ref, block_ref, *refs):
    own_ref, two_ref, near_ref, apart_ref, acc_ref = refs[-5:]
    acc_ref[...] = jnp.zeros_like(acc_ref)
    most = table_ref.shape[1]
    steps = tiles_ref.shape[0] // most
    col_tiles = own_ref.shape[0] // TILE
    for step in range(steps - 1, -1, -1):
        for k in range(most):
            col = pl.multiple_of(table_ref[steps + step, k] * TILE, TILE)
            quarter = table_ref[step, k] // col_tiles
            row = pl.multiple_of(table_ref[step, k] % col_tiles * TILE, TILE)
            live = (k < table_ref[2 * steps, step]).astype(F32)
            prod = dot(tiles_ref[step * most + k], block_ref[quarter, pl.ds(row, TILE), :])
            acc_ref[step, pl.ds(col, TILE), :] += prod * live
    odd = table_ref[2 * steps + 1, 0]
    own_ref[...] = acc_ref[0]
    two_ref[...] = acc_ref[2]
    near_ref[...] = acc_ref[1 + 2 * odd].astype(BF16)
    apart_ref[...] = acc_ref[3 - 2 * odd].astype(BF16)


def row_kernel(parts_ref, out_ref):
    count, width = parts_ref.shape
    pairs = jnp.sum(parts_ref[...].astype(F32).reshape(count // 8, 8, width), axis=0)
    out_ref[...] = jnp.concatenate([pairs[:4] + pairs[4:], jnp.zeros((4, width), F32)], axis=0)


def add_kernel(a_ref, b_ref, out_ref):
    out_ref[...] = (a_ref[...] + b_ref[...].astype(F32)).astype(BF16)


def slot_of(lines, dim):
    index = iota(lines, dim)
    owner = quotient(index, 12)
    return owner, index - 12 * owner


def back_kernel(own_ref, in1, in2, degree_ref, unplace_ref, terms_ref, out_ref):
    total = own_ref[...] + in1[...].astype(F32) + in2[...].astype(F32)
    grads = scaled_rows(degree_ref, total).astype(BF16)
    slots = dot(unplace_ref[...], grads).astype(BF16)
    empty = jnp.zeros((TILE - 8, terms_ref.shape[1]), F32)
    term = jnp.concatenate([terms_ref[...], empty], axis=0).astype(BF16)
    lines = (TILE // 8 * 12, TILE)
    owner, slot = slot_of(lines, 0)
    widen = one_hot((slot < 8) & (owner * 8 + slot == iota(lines, 1)))
    ends = dot(one_hot(slot == 8 + iota(lines, 1)), term)
    for t in range(slots.shape[0] // TILE):
        group = dot(widen, slots[t * TILE : (t + 1) * TILE]) + ends
        out_ref[t * lines[0] : (t + 1) * lines[0]] = group.astype(BF16)


def last_kernel(key_ref, returned_ref, out_ref, weight_ref, bias_ref):
    rows = out_ref.shape[0]
    owners = TILE // 8
    lines = (TILE + 3 * owners, 12 * owners)
    owner, slot = slot_of(lines, 1)
    row = iota(lines, 0)
    wanted = (slot < 8) & (owner * 8 + slot == row)
    wanted |= (slot == 8) & (owner + TILE == row)
    wanted |= (slot == 9) & (owner + TILE + owners == row)
    wanted |= ((slot == 10) & (row == TILE + 2 * owners)) | ((slot == 11) & (row == TILE + 2 * owners + 1))
    pick = one_hot(wanted)
    total = jnp.zeros((rows, TILE), F32)
    bias = jnp.zeros((owners, TILE), F32)
    for t in range(returned_ref.shape[0] // lines[1]):
        found = dot(pick, returned_ref[t * lines[1] : (t + 1) * lines[1]])
        span = slice(t * TILE, (t + 1) * TILE)
        here = one_hot(iota((rows, TILE), 0).astype(F32) == key_ref[0:1, span])
        total = total + dot(here, found[:TILE].astype(BF16))
        for k in range(2):
            part = found[TILE + k * owners : TILE + (k + 1) * owners]
            weight_ref[t * owners : (t + 1) * owners, k * TILE : (k + 1) * TILE] = part
        bias = bias + found[TILE + 2 * owners :]
    out_ref[...] = total.astype(BF16)
    bias_ref[:, :TILE] = bias[0:1]
    bias_ref[:, TILE:] = bias[1:2]


def moved(value, target):
    count = lax.axis_size("blk")
    return lax.ppermute(value, "blk", [(s, target(s) % count) for s in range(count)])


def two_on(blk):
    return blk + 2


def two_back(blk):
    return blk - 2


def apart_on(blk):
    return blk + 1 + 2 * (blk % 2)


def apart_back(blk):
    return blk - 3 + 2 * (blk % 2)


def other_core(blk):
    return blk + 1 - 2 * (blk % 2)


def exchange(value, axis):
    return lax.all_to_all(value, axis, split_axis=0, concat_axis=0, tiled=True)


def tile_call(kernel, outs, scratch, name, table, arrays, after=()):
    specs = [pl.BlockSpec(memory_space=pltpu.SMEM)]
    specs += [pl.BlockSpec(memory_space=pltpu.VMEM)] * len(arrays)
    specs += [pl.BlockSpec(memory_space=pl.ANY)] * len(after)
    return kernel_call(kernel, outs, specs, name, scratch)(table, *arrays, *after)


def on_device(
    features,
    send_rows,
    send_counts,
    tile_values,
    tile_rows,
    tile_cols,
    tile_counts,
    degree_scale,
    weight,
    bias,
    out_grad,
):
    blocks = lax.axis_size("blk")
    quarters = lax.axis_size("rep")
    rows, width = features.shape
    slots = send_rows.shape[1]
    steps, most = tile_values.shape[:2]
    hidden_width = weight.shape[1]
    total = blocks * slots
    slot_rows = send_rows.T
    counts_row = send_counts.reshape(1, blocks)
    degree = degree_scale.reshape(rows // TILE, TILE)
    tiles = tile_values.reshape(steps * most, TILE, TILE)
    tables = (tile_rows, tile_cols, tile_counts.reshape(1, steps))

    outgoing, scale, bias_row, table, key = start_call(
        features, slot_rows, counts_row, degree, tables, bias.reshape(1, hidden_width)
    )
    incoming = exchange(outgoing.reshape(blocks, slots, width), "blk").reshape(total, width)
    scaled = call(place_kernel, shape((rows, width), BF16), "place")(incoming, scale)
    two = moved(scaled, two_on)
    sources = (scaled, two, moved(scaled, apart_on), moved(two, other_core))
    unplace = call(unplace_kernel, shape((total, rows), BF16), "unplace", flops=10**8)(incoming)
    turned = call(transpose_kernel, shape(tiles.shape, BF16), "turn", flops=LONG)(
        tiles, after=(scaled,)
    )
    partial = tile_call(
        gather_kernel,
        shape((quarters, rows, width), BF16),
        [pltpu.VMEM((quarters * rows, width), F32)],
        "gather_tiles",
        table,
        (tiles, *sources),
        (turned, unplace),
    )
    parts = exchange(partial, "rep")
    hidden, sent = call(
        dense_kernel,
        (
            shape((rows, hidden_width), BF16),
            shape((quarters, rows + 2 * width + 16, width), BF16),
        ),
        "dense",
        (pltpu.VMEM((rows, width), BF16), pltpu.VMEM((rows, hidden_width), BF16)),
    )(parts, scale, weight, bias_row, out_grad)
    block = exchange(sent, "rep")
    terms = call(terms_kernel, shape((4 * width, TILE), BF16), "terms")(block)
    lines = terms
    terms = exchange(terms.reshape(blocks, 4, TILE), "blk").reshape(4 * width, TILE)

    own, two, near, apart = tile_call(
        spread_kernel,
        (shape((rows, width), F32),) * 2 + (shape((rows, width), BF16),) * 2,
        [pltpu.VMEM((steps, rows, width), F32)],
        "spread_tiles",
        table,
        (turned, block),
        (lines,),
    )
    near = moved(near, other_core)
    apart = moved(apart, apart_back)
    two = moved(call(add_kernel, shape((rows, width), BF16), "add")(two, near), two_back)
    terms = call(row_kernel, shape((8, TILE), F32), "row", flops=LONG)(terms)
    back = call(back_kernel, shape((blocks * (slots + 4), width), BF16), "back")(
        own, apart, two, scale, unplace, terms
    )
    returned = exchange(back.reshape(blocks, 3, 4, width), "blk").reshape(back.shape)
    grad_features, grad_weight, grad_bias = call(
        last_kernel,
        (shape((rows, width), BF16), shape(weight.shape, F32), shape((1, hidden_width), F32)),
        "last",
    )(key, returned)
    return (hidden, grad_features, grad_weight, grad_bias.reshape(hidden_width))


def solution(mesh):
    in_specs = (
        P(("blk", "rep"), None),
        P(("blk", "rep"), None),
        P(("blk", "rep")),
        P(("blk", "rep"), None, None, None),
        P(("blk", "rep"), None),
        P(("blk", "rep"), None),
        P(("blk", "rep")),
        P(("blk", "rep")),
        P(),
        P(),
        P(("blk", "rep"), None),
    )
    out_specs = (P(("blk", "rep"), None), P(("blk", "rep"), None), P(), P())
    return jax.shard_map(
        on_device, mesh=mesh, in_specs=in_specs, out_specs=out_specs, check_vma=False
    )
```

```python
import jax
import jax.numpy as jnp
from jax import lax
from jax.experimental import pallas as pl
from jax.experimental.pallas import tpu as pltpu
from jax.sharding import PartitionSpec as P

BF16 = jnp.bfloat16
F32 = jnp.float32
TILE = 128
LONG = 10**11
UNUSED = 1024.0
NN = (((1,), (0,)), ((), ()))
NT = (((1,), (1,)), ((), ()))
TN = (((0,), (0,)), ((), ()))


def dot(a, b, dims=NN):
    return lax.dot_general(a, b, dims, preferred_element_type=F32)


def iota(shape, dim):
    return lax.broadcasted_iota(jnp.int32, shape, dim)


def one_hot(mask):
    return jnp.where(mask, 1.0, 0.0).astype(BF16)


def kernel_call(kernel, outs, specs, name, scratch=(), flops=10**8):
    return pl.pallas_call(
        kernel,
        out_shape=outs,
        in_specs=specs,
        scratch_shapes=list(scratch),
        compiler_params=pltpu.CompilerParams(vmem_limit_bytes=16 * 1024 * 1024),
        cost_estimate=pl.CostEstimate(flops=flops, bytes_accessed=10**6, transcendentals=0),
        name=name,
    )


def call(kernel, outs, name, scratch=(), flops=10**8):
    def run(*arrays, after=()):
        specs = [pl.BlockSpec(memory_space=pltpu.VMEM)] * len(arrays)
        specs += [pl.BlockSpec(memory_space=pl.ANY)] * len(after)
        return kernel_call(kernel, outs, specs, name, scratch, flops)(*arrays, *after)

    return run


def shape(dims, kind):
    return jax.ShapeDtypeStruct(dims, kind)


def quotient(value, divisor):
    return jnp.floor((value.astype(F32) + 0.5) * (1.0 / divisor)).astype(jnp.int32)


def as_column(row):
    return jnp.transpose(jnp.broadcast_to(row, (TILE, TILE)))


def slot_parts(send_rows, counts, rows):
    send_rows = jnp.transpose(send_rows.astype(F32)).astype(jnp.int32)
    owners, slots = send_rows.shape
    count = as_column(counts.astype(F32))[:, :slots]
    lane = iota((owners, slots), 1).astype(F32)
    key = jnp.where(lane < count, send_rows, rows)
    high = (key >> 5).astype(F32).astype(BF16)
    low = (key & 31).astype(F32).astype(BF16)
    total = owners * slots
    expand = one_hot(quotient(iota((total, owners), 0), slots) == iota((total, owners), 1))
    row = iota((total, slots), 0)
    mine = row - quotient(row, slots) * slots == iota((total, slots), 1)
    high = jnp.where(mine, dot(expand, high) * 32.0, 0.0).astype(BF16)
    low = jnp.where(mine, dot(expand, low), 0.0).astype(BF16)
    return high, low


def start_kernel(*refs):
    out_ref, degree_ref, bias_ref, table_ref, key_ref = refs[8:13]
    features_ref, rows_ref, counts_ref, *parts, sems = refs[13:]
    pairs = tuple(zip(refs[:8], (features_ref, rows_ref, counts_ref, degree_ref, *parts, bias_ref)))
    copies = [pltpu.make_async_copy(a, b, sems.at[k]) for k, (a, b) in enumerate(pairs)]
    for copy in copies[1:]:
        copy.start()
    copies[0].start()
    copies[1].wait()
    copies[2].wait()
    rows = features_ref.shape[0]
    slots = rows_ref.shape[0]
    high, low = slot_parts(rows_ref[...], counts_ref[...], rows)
    ones = jnp.ones((slots, TILE), BF16)
    key = dot(high, ones) + dot(low, ones)
    lane = iota(key.shape, 1).astype(F32)
    pick = jnp.concatenate(
        [one_hot(key == lane + float(start)) for start in range(0, rows, TILE)], axis=1
    )
    copies[0].wait()
    sent = dot(pick, features_ref[...])
    out_ref[...] = jnp.where(key >= float(rows), UNUSED, sent).astype(BF16)
    ones = jnp.ones((8, slots), BF16)
    key_ref[...] = dot(ones, high, NT) + dot(ones, low, NT)
    for copy in copies[3:]:
        copy.wait()
    place = 0
    for part in parts:
        table_ref[place : place + part.shape[0]] = part[...]
        place += part.shape[0]
    odd = lax.rem(lax.axis_index("blk"), 2)
    table_ref[place : place + 1] = jnp.full((1, table_ref.shape[1]), odd, jnp.int32)


def start_call(features, send_rows, counts_row, degree, tables, bias_row):
    rows, width = features.shape
    total = send_rows.size
    small = (features, send_rows, counts_row, degree, *tables)
    arrays = [pltpu.with_memory_space_constraint(a, pltpu.HBM) for a in (*small, bias_row)]
    return pl.pallas_call(
        start_kernel,
        out_shape=(
            shape((total, width), BF16),
            shape(degree.shape, F32),
            shape(bias_row.shape, F32),
            shape((1 + sum(a.shape[0] for a in tables), tables[0].shape[1]), jnp.int32),
            shape((8, total), F32),
        ),
        in_specs=[pl.BlockSpec(memory_space=pltpu.HBM)] * 8,
        scratch_shapes=[pltpu.VMEM(a.shape, a.dtype) for a in (features, send_rows, counts_row, *tables)]
        + [pltpu.SemaphoreType.DMA((8,))],
        compiler_params=pltpu.CompilerParams(vmem_limit_bytes=8 * 1024 * 1024),
        cost_estimate=pl.CostEstimate(flops=10**8, bytes_accessed=10**6, transcendentals=0),
        name="start",
    )(*arrays)


def transpose_kernel(tiles_ref, *refs):
    out_ref = refs[-1]
    for t in range(tiles_ref.shape[0]):
        out_ref[t] = jnp.transpose(tiles_ref[t].astype(F32)).astype(BF16)


def used_slots(ref):
    return jnp.where(ref[...].astype(F32) < 512.0, 1.0, 0.0).astype(BF16)


def scaled_rows(degree_ref, values):
    count = values.shape[0] // TILE
    parts = [
        as_column(degree_ref[t : t + 1]) * values[t * TILE : (t + 1) * TILE] for t in range(count)
    ]
    return jnp.concatenate(parts, axis=0)


def place_kernel(incoming_ref, degree_ref, out_ref):
    rows = out_ref.shape[0]
    used = used_slots(incoming_ref)
    before = one_hot(iota((TILE, TILE), 0) < iota((TILE, TILE), 1))
    ones = jnp.ones((TILE, TILE), BF16)
    mean = jnp.full((8, TILE), 1.0 / TILE, BF16)
    offset = jnp.zeros((8, TILE), F32)
    parts = []
    for start in range(0, used.shape[0], TILE):
        here = dot(mean, used[start : start + TILE], NT)
        flags = here.astype(BF16)
        rank = jnp.where(here > 0.5, dot(flags, before) + offset, -1.0)
        offset = offset + dot(flags, ones)
        parts.append(one_hot(iota((rows, TILE), 0).astype(F32) == rank[0:1]))
    owned = dot(jnp.concatenate(parts, axis=1), incoming_ref[...])
    out_ref[...] = scaled_rows(degree_ref, owned).astype(BF16)


def unplace_kernel(incoming_ref, out_ref):
    rows = out_ref.shape[1]
    used = used_slots(incoming_ref)
    before = one_hot(iota((TILE, TILE), 1) < iota((TILE, TILE), 0))
    ones = jnp.ones((TILE, TILE), BF16)
    offset = jnp.zeros((TILE, TILE), F32)
    lane = iota((TILE, TILE), 1).astype(F32)
    for start in range(0, used.shape[0], TILE):
        here = used[start : start + TILE]
        rank = jnp.where(here.astype(F32) > 0.5, dot(before, here) + offset, -1.0)
        offset = offset + dot(ones, here)
        for column in range(0, rows, TILE):
            out_ref[start : start + TILE, column : column + TILE] = one_hot(
                rank == lane + float(column)
            )


def gather_kernel(table_ref, tiles_ref, src0, two, apart, near, *refs):
    out_ref, acc_ref = refs[-2:]
    acc_ref[...] = jnp.zeros_like(acc_ref)
    most = table_ref.shape[1]
    steps = tiles_ref.shape[0] // most
    odd = table_ref[2 * steps + 1, 0]
    for step, source in ((0, src0), (2, two), (3 - 2 * odd, apart), (1 + 2 * odd, near)):
        for k in range(most):
            col = pl.multiple_of(table_ref[steps + step, k] * TILE, TILE)
            row = pl.multiple_of(table_ref[step, k] * TILE, TILE)
            live = (k < table_ref[2 * steps, step]).astype(F32)
            prod = dot(tiles_ref[step * most + k], source[pl.ds(col, TILE), :])
            acc_ref[pl.ds(row, TILE), :] += prod * live
    quarters, rows, _ = out_ref.shape
    for q in range(quarters):
        out_ref[q] = acc_ref[q * rows : (q + 1) * rows].astype(BF16)


def dense_kernel(
    parts_ref, degree_ref, weight_ref, bias_ref, out_grad_ref, hidden_ref, out_ref, agg_ref, grad_pre_ref
):
    quarters, rows, width = parts_ref.shape
    summed = parts_ref[0].astype(F32)
    for q in range(1, quarters):
        summed = summed + parts_ref[q].astype(F32)
    for t in range(rows // TILE):
        part = slice(t * TILE, (t + 1) * TILE)
        scale = as_column(degree_ref[t : t + 1])
        agg = (scale * summed[part]).astype(BF16)
        agg_ref[part] = agg
        pre = dot(agg, weight_ref[...]) + bias_ref[...]
        sig = jax.nn.sigmoid(pre)
        hidden_ref[part] = (pre * sig).astype(BF16)
        grad_pre = (
            out_grad_ref[part].astype(F32) * (sig * (1.0 + pre * (1.0 - sig)))
        ).astype(BF16)
        grad_pre_ref[part] = grad_pre
        grad_agg = (scale * dot(grad_pre, weight_ref[...], NT)).astype(BF16)
        for q in range(quarters):
            out_ref[q, part] = grad_agg
    grad_pre = grad_pre_ref[...]
    term = dot(agg_ref[...], grad_pre, TN).astype(BF16)
    total = jnp.sum(grad_pre.astype(F32), axis=0, keepdims=True)
    high = total.astype(BF16).astype(F32)
    pieces = (high[:, :TILE], high[:, TILE:], (total - high)[:, :TILE], (total - high)[:, TILE:])
    row = iota((16, TILE), 0)
    ends = jnp.zeros((16, TILE), F32)
    for k, piece in enumerate(pieces):
        ends = jnp.where(row == k, piece, ends)
    for q in range(quarters):
        out_ref[q, rows : rows + width] = term[:, :TILE]
        out_ref[q, rows + width : rows + 2 * width] = term[:, TILE:]
        out_ref[q, rows + 2 * width :] = ends.astype(BF16)


def terms_halves(block_ref):
    quarters, all_rows, width = block_ref.shape
    rows = all_rows - 2 * width - 16
    total = block_ref[0, rows:].astype(F32)
    for q in range(1, quarters):
        total = total + block_ref[q, rows:].astype(F32)
    ends = total[2 * width :]
    half = width // 2
    lines = (4 * half, half)
    out = [jnp.zeros((4 * half, TILE), F32) for _ in range(2)]
    for k in range(4):
        if k < 2:
            piece = total[k * width : (k + 1) * width]
        else:
            bias = ends[k - 2 : k - 1] + ends[k : k + 1]
            mine = (iota((width, TILE), 1) + (k - 2) * TILE) // 2 == iota((width, TILE), 0)
            piece = jnp.where(mine, bias, 0.0)
        here = one_hot(iota(lines, 0) == 4 * iota(lines, 1) + k)
        piece = piece.astype(BF16)
        out = [out[h] + dot(here, piece[h * half : (h + 1) * half]) for h in range(2)]
    return out


def spread_kernel(table_ref, tiles_ref, block_ref, *refs):
    own_ref, two_ref, near_ref, apart_ref, mine_ref, acc_ref = refs
    acc_ref[...] = jnp.zeros_like(acc_ref)
    most = table_ref.shape[1]
    steps = tiles_ref.shape[0] // most
    col_tiles = own_ref.shape[0] // TILE
    for step in range(steps - 1, -1, -1):
        for k in range(most):
            col = pl.multiple_of(table_ref[steps + step, k] * TILE, TILE)
            quarter = table_ref[step, k] // col_tiles
            row = pl.multiple_of(table_ref[step, k] % col_tiles * TILE, TILE)
            live = (k < table_ref[2 * steps, step]).astype(F32)
            prod = dot(tiles_ref[step * most + k], block_ref[quarter, pl.ds(row, TILE), :])
            acc_ref[step, pl.ds(col, TILE), :] += prod * live
    odd = table_ref[2 * steps + 1, 0]
    own_ref[...] = acc_ref[0]
    two_ref[...] = acc_ref[2]
    rows = own_ref.shape[0]
    near_ref[:rows] = acc_ref[1 + 2 * odd].astype(BF16)
    first, second = terms_halves(block_ref)
    mine_ref[...] = jnp.where(odd == 0, first, second)
    near_ref[rows:] = jnp.where(odd == 0, second, first).astype(BF16)
    apart_ref[...] = acc_ref[3 - 2 * odd].astype(BF16)


def row_kernel(parts_ref, out_ref):
    count, width = parts_ref.shape
    pairs = jnp.sum(parts_ref[...].astype(F32).reshape(count // 8, 8, width), axis=0)
    out_ref[...] = jnp.concatenate([pairs[:4] + pairs[4:], jnp.zeros((4, width), F32)], axis=0)


def add_kernel(two_ref, mine_ref, near_ref, out_ref, terms_ref):
    rows = out_ref.shape[0]
    out_ref[...] = (two_ref[...] + near_ref[:rows].astype(F32)).astype(BF16)
    terms_ref[...] = (mine_ref[...] + near_ref[rows:].astype(F32)).astype(BF16)


def slot_of(lines, dim):
    index = iota(lines, dim)
    owner = quotient(index, 12)
    return owner, index - 12 * owner


def back_kernel(own_ref, in1, in2, degree_ref, unplace_ref, terms_ref, out_ref):
    total = own_ref[...] + in1[...].astype(F32) + in2[...].astype(F32)
    grads = scaled_rows(degree_ref, total).astype(BF16)
    slots = dot(unplace_ref[...], grads).astype(BF16)
    empty = jnp.zeros((TILE - 8, terms_ref.shape[1]), F32)
    term = jnp.concatenate([terms_ref[...], empty], axis=0).astype(BF16)
    lines = (TILE // 8 * 12, TILE)
    owner, slot = slot_of(lines, 0)
    widen = one_hot((slot < 8) & (owner * 8 + slot == iota(lines, 1)))
    ends = dot(one_hot(slot == 8 + iota(lines, 1)), term)
    for t in range(slots.shape[0] // TILE):
        group = dot(widen, slots[t * TILE : (t + 1) * TILE]) + ends
        out_ref[t * lines[0] : (t + 1) * lines[0]] = group.astype(BF16)


def last_kernel(key_ref, returned_ref, out_ref, weight_ref, bias_ref):
    rows = out_ref.shape[0]
    owners = TILE // 8
    lines = (TILE + 3 * owners, 12 * owners)
    owner, slot = slot_of(lines, 1)
    row = iota(lines, 0)
    wanted = (slot < 8) & (owner * 8 + slot == row)
    place = TILE + owner % 2 * (owners // 2) + owner // 2
    wanted |= ((slot == 8) & (place == row)) | ((slot == 9) & (place + owners == row))
    wanted |= ((slot == 10) & (row == TILE + 2 * owners)) | ((slot == 11) & (row == TILE + 2 * owners + 1))
    pick = one_hot(wanted)
    total = jnp.zeros((rows, TILE), F32)
    bias = jnp.zeros((owners, TILE), F32)
    for t in range(returned_ref.shape[0] // lines[1]):
        found = dot(pick, returned_ref[t * lines[1] : (t + 1) * lines[1]])
        span = slice(t * TILE, (t + 1) * TILE)
        here = one_hot(iota((rows, TILE), 0).astype(F32) == key_ref[0:1, span])
        total = total + dot(here, found[:TILE].astype(BF16))
        for k in range(2):
            for core in range(2):
                start = TILE + (2 * k + core) * (owners // 2)
                line = core * (weight_ref.shape[0] // 2) + t * (owners // 2)
                part = found[start : start + owners // 2]
                weight_ref[line : line + owners // 2, k * TILE : (k + 1) * TILE] = part
        bias = bias + found[TILE + 2 * owners :]
    out_ref[...] = total.astype(BF16)
    bias_ref[:, :TILE] = bias[0:1]
    bias_ref[:, TILE:] = bias[1:2]


def moved(value, target):
    count = lax.axis_size("blk")
    return lax.ppermute(value, "blk", [(s, target(s) % count) for s in range(count)])


def two_on(blk):
    return blk + 2


def two_back(blk):
    return blk - 2


def apart_on(blk):
    return blk + 1 + 2 * (blk % 2)


def apart_back(blk):
    return blk - 3 + 2 * (blk % 2)


def other_core(blk):
    return blk + 1 - 2 * (blk % 2)


def exchange(value, axis, groups=None):
    return lax.all_to_all(
        value, axis, split_axis=0, concat_axis=0, axis_index_groups=groups, tiled=True
    )


def tile_call(kernel, outs, scratch, name, table, arrays, after=()):
    specs = [pl.BlockSpec(memory_space=pltpu.SMEM)]
    specs += [pl.BlockSpec(memory_space=pltpu.VMEM)] * len(arrays)
    specs += [pl.BlockSpec(memory_space=pl.ANY)] * len(after)
    return kernel_call(kernel, outs, specs, name, scratch)(table, *arrays, *after)


def on_device(
    features,
    send_rows,
    send_counts,
    tile_values,
    tile_rows,
    tile_cols,
    tile_counts,
    degree_scale,
    weight,
    bias,
    out_grad,
):
    blocks = lax.axis_size("blk")
    quarters = lax.axis_size("rep")
    rows, width = features.shape
    slots = send_rows.shape[1]
    steps, most = tile_values.shape[:2]
    hidden_width = weight.shape[1]
    total = blocks * slots
    slot_rows = send_rows.T
    counts_row = send_counts.reshape(1, blocks)
    degree = degree_scale.reshape(rows // TILE, TILE)
    tiles = tile_values.reshape(steps * most, TILE, TILE)
    tables = (tile_rows, tile_cols, tile_counts.reshape(1, steps))

    outgoing, scale, bias_row, table, key = start_call(
        features, slot_rows, counts_row, degree, tables, bias.reshape(1, hidden_width)
    )
    incoming = exchange(outgoing.reshape(blocks, slots, width), "blk").reshape(total, width)
    scaled = call(place_kernel, shape((rows, width), BF16), "place")(incoming, scale)
    two = moved(scaled, two_on)
    sources = (scaled, two, moved(scaled, apart_on), moved(two, other_core))
    unplace = call(unplace_kernel, shape((total, rows), BF16), "unplace", flops=10**8)(incoming)
    turned = call(transpose_kernel, shape(tiles.shape, BF16), "turn", flops=LONG)(
        tiles, after=(scaled,)
    )
    partial = tile_call(
        gather_kernel,
        shape((quarters, rows, width), BF16),
        [pltpu.VMEM((quarters * rows, width), F32)],
        "gather_tiles",
        table,
        (tiles, *sources),
        (turned, unplace),
    )
    parts = exchange(partial, "rep")
    hidden, sent = call(
        dense_kernel,
        (
            shape((rows, hidden_width), BF16),
            shape((quarters, rows + 2 * width + 16, width), BF16),
        ),
        "dense",
        (pltpu.VMEM((rows, width), BF16), pltpu.VMEM((rows, hidden_width), BF16)),
    )(parts, scale, weight, bias_row, out_grad)
    block = exchange(sent, "rep")
    own, two, near, apart, mine = tile_call(
        spread_kernel,
        (
            shape((rows, width), F32),
            shape((rows, width), F32),
            shape((rows + 2 * width, width), BF16),
            shape((rows, width), BF16),
            shape((2 * width, width), F32),
        ),
        [pltpu.VMEM((steps, rows, width), F32)],
        "spread_tiles",
        table,
        (turned, block),
    )
    near = moved(near, other_core)
    apart = moved(apart, apart_back)
    two, terms = call(
        add_kernel, (shape((rows, width), BF16), shape((2 * width, width), BF16)), "add"
    )(two, mine, near)
    two = moved(two, two_back)
    cores = [list(range(core, blocks, 2)) for core in range(2)]
    terms = exchange(terms.reshape(blocks // 2, 4, width), "blk", cores).reshape(terms.shape)
    terms = call(row_kernel, shape((8, TILE), F32), "row", flops=LONG)(terms)
    back = call(back_kernel, shape((blocks * (slots + 4), width), BF16), "back")(
        own, apart, two, scale, unplace, terms
    )
    returned = exchange(back.reshape(blocks, 3, 4, width), "blk").reshape(back.shape)
    grad_features, grad_weight, grad_bias = call(
        last_kernel,
        (shape((rows, width), BF16), shape(weight.shape, F32), shape((1, hidden_width), F32)),
        "last",
    )(key, returned)
    return (hidden, grad_features, grad_weight, grad_bias.reshape(hidden_width))


def solution(mesh):
    in_specs = (
        P(("blk", "rep"), None),
        P(("blk", "rep"), None),
        P(("blk", "rep")),
        P(("blk", "rep"), None, None, None),
        P(("blk", "rep"), None),
        P(("blk", "rep"), None),
        P(("blk", "rep")),
        P(("blk", "rep")),
        P(),
        P(),
        P(("blk", "rep"), None),
    )
    out_specs = (P(("blk", "rep"), None), P(("blk", "rep"), None), P(), P())
    return jax.shard_map(
        on_device, mesh=mesh, in_specs=in_specs, out_specs=out_specs, check_vma=False
    )
```

```python
import jax
import jax.numpy as jnp
from jax import lax
from jax.experimental import pallas as pl
from jax.experimental.pallas import tpu as pltpu
from jax.sharding import PartitionSpec as P

BF16 = jnp.bfloat16
F32 = jnp.float32
TILE = 128
LONG = 10**11
UNUSED = 1024.0
NN = (((1,), (0,)), ((), ()))
NT = (((1,), (1,)), ((), ()))
TN = (((0,), (0,)), ((), ()))


def dot(a, b, dims=NN):
    return lax.dot_general(a, b, dims, preferred_element_type=F32)


def iota(shape, dim):
    return lax.broadcasted_iota(jnp.int32, shape, dim)


def one_hot(mask):
    return jnp.where(mask, 1.0, 0.0).astype(BF16)


def kernel_call(kernel, outs, specs, name, scratch=(), flops=10**8):
    return pl.pallas_call(
        kernel,
        out_shape=outs,
        in_specs=specs,
        scratch_shapes=list(scratch),
        compiler_params=pltpu.CompilerParams(vmem_limit_bytes=16 * 1024 * 1024),
        cost_estimate=pl.CostEstimate(flops=flops, bytes_accessed=10**6, transcendentals=0),
        name=name,
    )


def call(kernel, outs, name, scratch=(), flops=10**8):
    def run(*arrays, after=()):
        specs = [pl.BlockSpec(memory_space=pltpu.VMEM)] * len(arrays)
        specs += [pl.BlockSpec(memory_space=pl.ANY)] * len(after)
        return kernel_call(kernel, outs, specs, name, scratch, flops)(*arrays, *after)

    return run


def shape(dims, kind):
    return jax.ShapeDtypeStruct(dims, kind)


def quotient(value, divisor):
    return jnp.floor((value.astype(F32) + 0.5) * (1.0 / divisor)).astype(jnp.int32)


def as_column(row):
    return jnp.transpose(jnp.broadcast_to(row, (TILE, TILE)))


def slot_parts(send_rows, counts, rows):
    send_rows = jnp.transpose(send_rows.astype(F32)).astype(jnp.int32)
    owners, slots = send_rows.shape
    count = as_column(counts.astype(F32))[:, :slots]
    lane = iota((owners, slots), 1).astype(F32)
    key = jnp.where(lane < count, send_rows, rows)
    high = (key >> 5).astype(F32).astype(BF16)
    low = (key & 31).astype(F32).astype(BF16)
    total = owners * slots
    expand = one_hot(iota((total, owners), 0) // slots == iota((total, owners), 1))
    mine = iota((total, slots), 0) % slots == iota((total, slots), 1)
    high = jnp.where(mine, dot(expand, high) * 32.0, 0.0).astype(BF16)
    low = jnp.where(mine, dot(expand, low), 0.0).astype(BF16)
    return high, low


def start_kernel(*refs):
    out_ref, degree_ref, bias_ref, table_ref, rows_ref, counts_ref = refs[8:14]
    features_ref, *parts, sems = refs[14:]
    pairs = tuple(zip(refs[:8], (features_ref, rows_ref, counts_ref, degree_ref, *parts, bias_ref)))
    copies = [pltpu.make_async_copy(a, b, sems.at[k]) for k, (a, b) in enumerate(pairs)]
    for copy in copies:
        copy.start()
    copies[1].wait()
    copies[2].wait()
    rows = features_ref.shape[0]
    slots = rows_ref.shape[0]
    high, low = slot_parts(rows_ref[...], counts_ref[...], rows)
    ones = jnp.ones((slots, TILE), BF16)
    key = dot(high, ones) + dot(low, ones)
    lane = iota(key.shape, 1).astype(F32)
    pick = jnp.concatenate(
        [one_hot(key == lane + float(start)) for start in range(0, rows, TILE)], axis=1
    )
    copies[0].wait()
    sent = dot(pick, features_ref[...])
    out_ref[...] = jnp.where(key >= float(rows), UNUSED, sent).astype(BF16)
    for copy in copies[3:]:
        copy.wait()
    place = 0
    for part in parts:
        table_ref[place : place + part.shape[0]] = part[...]
        place += part.shape[0]
    odd = lax.rem(lax.axis_index("blk"), 2)
    table_ref[place : place + 1] = jnp.full((1, table_ref.shape[1]), odd, jnp.int32)


def start_call(features, send_rows, counts_row, degree, tables, bias_row):
    rows, width = features.shape
    total = send_rows.size
    small = (features, send_rows, counts_row, degree, *tables)
    arrays = [pltpu.with_memory_space_constraint(a, pltpu.HBM) for a in (*small, bias_row)]
    return pl.pallas_call(
        start_kernel,
        out_shape=(
            shape((total, width), BF16),
            shape(degree.shape, F32),
            shape(bias_row.shape, F32),
            shape((1 + sum(a.shape[0] for a in tables), tables[0].shape[1]), jnp.int32),
            shape(send_rows.shape, jnp.int32),
            shape(counts_row.shape, jnp.int32),
        ),
        in_specs=[pl.BlockSpec(memory_space=pltpu.HBM)] * 8,
        scratch_shapes=[pltpu.VMEM(a.shape, a.dtype) for a in (features, *tables)]
        + [pltpu.SemaphoreType.DMA((8,))],
        compiler_params=pltpu.CompilerParams(vmem_limit_bytes=8 * 1024 * 1024),
        cost_estimate=pl.CostEstimate(flops=10**8, bytes_accessed=10**6, transcendentals=0),
        name="start",
    )(*arrays)


def arrive_kernel(rows_ref, counts_ref, *refs):
    out_ref = refs[-1]
    rows = out_ref.shape[0]
    high, low = slot_parts(rows_ref[...], counts_ref[...], rows)
    ones = jnp.ones((8, rows_ref.shape[0]), BF16)
    key = dot(ones, high, NT) + dot(ones, low, NT)
    for start in range(0, key.shape[1], TILE):
        span = slice(start, start + TILE)
        out_ref[:, span] = one_hot(iota((rows, TILE), 0).astype(F32) == key[0:1, span])


def transpose_kernel(tiles_ref, *refs):
    out_ref = refs[-1]
    for t in range(tiles_ref.shape[0]):
        out_ref[t] = jnp.transpose(tiles_ref[t].astype(F32)).astype(BF16)


def used_slots(ref):
    return jnp.where(ref[...].astype(F32) < 512.0, 1.0, 0.0).astype(BF16)


def scaled_rows(degree_ref, values):
    count = values.shape[0] // TILE
    parts = [
        as_column(degree_ref[t : t + 1]) * values[t * TILE : (t + 1) * TILE] for t in range(count)
    ]
    return jnp.concatenate(parts, axis=0)


def place_kernel(incoming_ref, degree_ref, out_ref):
    rows = out_ref.shape[0]
    used = used_slots(incoming_ref)
    before = one_hot(iota((TILE, TILE), 0) < iota((TILE, TILE), 1))
    ones = jnp.ones((TILE, TILE), BF16)
    mean = jnp.full((8, TILE), 1.0 / TILE, BF16)
    offset = jnp.zeros((8, TILE), F32)
    parts = []
    for start in range(0, used.shape[0], TILE):
        here = dot(mean, used[start : start + TILE], NT)
        flags = here.astype(BF16)
        rank = jnp.where(here > 0.5, dot(flags, before) + offset, -1.0)
        offset = offset + dot(flags, ones)
        parts.append(one_hot(iota((rows, TILE), 0).astype(F32) == rank[0:1]))
    owned = dot(jnp.concatenate(parts, axis=1), incoming_ref[...])
    out_ref[...] = scaled_rows(degree_ref, owned).astype(BF16)


def unplace_kernel(incoming_ref, out_ref):
    rows = out_ref.shape[1]
    used = used_slots(incoming_ref)
    before = one_hot(iota((TILE, TILE), 1) < iota((TILE, TILE), 0))
    ones = jnp.ones((TILE, TILE), BF16)
    offset = jnp.zeros((TILE, TILE), F32)
    lane = iota((TILE, TILE), 1).astype(F32)
    for start in range(0, used.shape[0], TILE):
        here = used[start : start + TILE]
        rank = jnp.where(here.astype(F32) > 0.5, dot(before, here) + offset, -1.0)
        offset = offset + dot(ones, here)
        for column in range(0, rows, TILE):
            out_ref[start : start + TILE, column : column + TILE] = one_hot(
                rank == lane + float(column)
            )


def gather_kernel(table_ref, tiles_ref, src0, two, apart, near, *refs):
    out_ref, acc_ref = refs[-2:]
    acc_ref[...] = jnp.zeros_like(acc_ref)
    most = table_ref.shape[1]
    steps = tiles_ref.shape[0] // most
    odd = table_ref[2 * steps + 1, 0]
    for step, source in ((0, src0), (2, two), (3 - 2 * odd, apart), (1 + 2 * odd, near)):
        for k in range(most):
            col = pl.multiple_of(table_ref[steps + step, k] * TILE, TILE)
            row = pl.multiple_of(table_ref[step, k] * TILE, TILE)
            live = (k < table_ref[2 * steps, step]).astype(F32)
            prod = dot(tiles_ref[step * most + k], source[pl.ds(col, TILE), :])
            acc_ref[pl.ds(row, TILE), :] += prod * live
    quarters, rows, _ = out_ref.shape
    for q in range(quarters):
        out_ref[q] = acc_ref[q * rows : (q + 1) * rows].astype(BF16)


def dense_kernel(
    parts_ref, degree_ref, weight_ref, bias_ref, out_grad_ref, hidden_ref, out_ref, agg_ref, grad_pre_ref
):
    quarters, rows, width = parts_ref.shape
    summed = parts_ref[0].astype(F32)
    for q in range(1, quarters):
        summed = summed + parts_ref[q].astype(F32)
    for t in range(rows // TILE):
        part = slice(t * TILE, (t + 1) * TILE)
        scale = as_column(degree_ref[t : t + 1])
        agg = (scale * summed[part]).astype(BF16)
        agg_ref[part] = agg
        pre = dot(agg, weight_ref[...]) + bias_ref[...]
        sig = jax.nn.sigmoid(pre)
        hidden_ref[part] = (pre * sig).astype(BF16)
        grad_pre = (
            out_grad_ref[part].astype(F32) * (sig * (1.0 + pre * (1.0 - sig)))
        ).astype(BF16)
        grad_pre_ref[part] = grad_pre
        grad_agg = (scale * dot(grad_pre, weight_ref[...], NT)).astype(BF16)
        for q in range(quarters):
            out_ref[q, part] = grad_agg
    grad_pre = grad_pre_ref[...]
    term = dot(agg_ref[...], grad_pre, TN).astype(BF16)
    total = jnp.sum(grad_pre.astype(F32), axis=0, keepdims=True)
    high = total.astype(BF16).astype(F32)
    pieces = (high[:, :TILE], high[:, TILE:], (total - high)[:, :TILE], (total - high)[:, TILE:])
    row = iota((16, TILE), 0)
    ends = jnp.zeros((16, TILE), F32)
    for k, piece in enumerate(pieces):
        ends = jnp.where(row == k, piece, ends)
    for q in range(quarters):
        out_ref[q, rows : rows + width] = term[:, :TILE]
        out_ref[q, rows + width : rows + 2 * width] = term[:, TILE:]
        out_ref[q, rows + 2 * width :] = ends.astype(BF16)


def terms_halves(block_ref):
    quarters, all_rows, width = block_ref.shape
    rows = all_rows - 2 * width - 16
    total = block_ref[0, rows:].astype(F32)
    for q in range(1, quarters):
        total = total + block_ref[q, rows:].astype(F32)
    ends = total[2 * width :]
    half = width // 2
    lines = (4 * half, half)
    out = [jnp.zeros((4 * half, TILE), F32) for _ in range(2)]
    for k in range(4):
        if k < 2:
            piece = total[k * width : (k + 1) * width]
        else:
            bias = ends[k - 2 : k - 1] + ends[k : k + 1]
            mine = (iota((width, TILE), 1) + (k - 2) * TILE) // 2 == iota((width, TILE), 0)
            piece = jnp.where(mine, bias, 0.0)
        here = one_hot(iota(lines, 0) == 4 * iota(lines, 1) + k)
        piece = piece.astype(BF16)
        out = [out[h] + dot(here, piece[h * half : (h + 1) * half]) for h in range(2)]
    return out


def spread_kernel(table_ref, tiles_ref, block_ref, *refs):
    own_ref, two_ref, near_ref, apart_ref, mine_ref, acc_ref = refs
    acc_ref[...] = jnp.zeros_like(acc_ref)
    most = table_ref.shape[1]
    steps = tiles_ref.shape[0] // most
    col_tiles = own_ref.shape[0] // TILE
    for step in range(steps - 1, -1, -1):
        for k in range(most):
            col = pl.multiple_of(table_ref[steps + step, k] * TILE, TILE)
            quarter = table_ref[step, k] // col_tiles
            row = pl.multiple_of(table_ref[step, k] % col_tiles * TILE, TILE)
            live = (k < table_ref[2 * steps, step]).astype(F32)
            prod = dot(tiles_ref[step * most + k], block_ref[quarter, pl.ds(row, TILE), :])
            acc_ref[step, pl.ds(col, TILE), :] += prod * live
    odd = table_ref[2 * steps + 1, 0]
    own_ref[...] = acc_ref[0]
    two_ref[...] = acc_ref[2]
    rows = own_ref.shape[0]
    near_ref[:rows] = acc_ref[1 + 2 * odd].astype(BF16)
    first, second = terms_halves(block_ref)
    mine_ref[...] = jnp.where(odd == 0, first, second)
    near_ref[rows:] = jnp.where(odd == 0, second, first).astype(BF16)
    apart_ref[...] = acc_ref[3 - 2 * odd].astype(BF16)


def add_kernel(two_ref, mine_ref, near_ref, out_ref, terms_ref):
    rows = out_ref.shape[0]
    out_ref[...] = (two_ref[...] + near_ref[:rows].astype(F32)).astype(BF16)
    terms_ref[...] = (mine_ref[...] + near_ref[rows:].astype(F32)).astype(BF16)


def slot_of(lines, dim):
    index = iota(lines, dim)
    owner = quotient(index, 12)
    return owner, index - 12 * owner


def back_kernel(own_ref, in1, in2, degree_ref, unplace_ref, terms_ref, *refs):
    out_ref = refs[-1]
    total = own_ref[...] + in1[...].astype(F32) + in2[...].astype(F32)
    grads = scaled_rows(degree_ref, total).astype(BF16)
    slots = dot(unplace_ref[...], grads).astype(BF16)
    count, width = terms_ref.shape
    pairs = jnp.sum(terms_ref[...].astype(F32).reshape(count // 8, 8, width), axis=0)
    term = jnp.concatenate([pairs[:4] + pairs[4:], jnp.zeros((TILE - 4, width), F32)], axis=0)
    term = term.astype(BF16)
    lines = (TILE // 8 * 12, TILE)
    owner, slot = slot_of(lines, 0)
    widen = one_hot((slot < 8) & (owner * 8 + slot == iota(lines, 1)))
    ends = dot(one_hot(slot == 8 + iota(lines, 1)), term)
    for t in range(slots.shape[0] // TILE):
        group = dot(widen, slots[t * TILE : (t + 1) * TILE]) + ends
        out_ref[t * lines[0] : (t + 1) * lines[0]] = group.astype(BF16)


def last_kernel(arrive_ref, returned_ref, out_ref, weight_ref, bias_ref):
    rows = out_ref.shape[0]
    owners = TILE // 8
    lines = (TILE + 3 * owners, 12 * owners)
    owner, slot = slot_of(lines, 1)
    row = iota(lines, 0)
    wanted = (slot < 8) & (owner * 8 + slot == row)
    place = TILE + owner % 2 * (owners // 2) + owner // 2
    wanted |= ((slot == 8) & (place == row)) | ((slot == 9) & (place + owners == row))
    wanted |= ((slot == 10) & (row == TILE + 2 * owners)) | ((slot == 11) & (row == TILE + 2 * owners + 1))
    pick = one_hot(wanted)
    total = jnp.zeros((rows, TILE), F32)
    bias = jnp.zeros((owners, TILE), F32)
    for t in range(returned_ref.shape[0] // lines[1]):
        found = dot(pick, returned_ref[t * lines[1] : (t + 1) * lines[1]])
        span = slice(t * TILE, (t + 1) * TILE)
        total = total + dot(arrive_ref[:, span], found[:TILE].astype(BF16))
        for k in range(2):
            for core in range(2):
                start = TILE + (2 * k + core) * (owners // 2)
                line = core * (weight_ref.shape[0] // 2) + t * (owners // 2)
                part = found[start : start + owners // 2]
                weight_ref[line : line + owners // 2, k * TILE : (k + 1) * TILE] = part
        bias = bias + found[TILE + 2 * owners :]
    out_ref[...] = total.astype(BF16)
    bias_ref[:, :TILE] = bias[0:1]
    bias_ref[:, TILE:] = bias[1:2]


def moved(value, target):
    count = lax.axis_size("blk")
    return lax.ppermute(value, "blk", [(s, target(s) % count) for s in range(count)])


def two_on(blk):
    return blk + 2


def two_back(blk):
    return blk - 2


def apart_on(blk):
    return blk + 1 + 2 * (blk % 2)


def apart_back(blk):
    return blk - 3 + 2 * (blk % 2)


def other_core(blk):
    return blk + 1 - 2 * (blk % 2)


def exchange(value, axis, groups=None):
    return lax.all_to_all(
        value, axis, split_axis=0, concat_axis=0, axis_index_groups=groups, tiled=True
    )


def tile_call(kernel, outs, scratch, name, table, arrays, after=()):
    specs = [pl.BlockSpec(memory_space=pltpu.SMEM)]
    specs += [pl.BlockSpec(memory_space=pltpu.VMEM)] * len(arrays)
    specs += [pl.BlockSpec(memory_space=pl.ANY)] * len(after)
    return kernel_call(kernel, outs, specs, name, scratch)(table, *arrays, *after)


def on_device(
    features,
    send_rows,
    send_counts,
    tile_values,
    tile_rows,
    tile_cols,
    tile_counts,
    degree_scale,
    weight,
    bias,
    out_grad,
):
    blocks = lax.axis_size("blk")
    quarters = lax.axis_size("rep")
    rows, width = features.shape
    slots = send_rows.shape[1]
    steps, most = tile_values.shape[:2]
    hidden_width = weight.shape[1]
    total = blocks * slots
    slot_rows = send_rows.T
    counts_row = send_counts.reshape(1, blocks)
    degree = degree_scale.reshape(rows // TILE, TILE)
    tiles = tile_values.reshape(steps * most, TILE, TILE)
    tables = (tile_rows, tile_cols, tile_counts.reshape(1, steps))

    outgoing, scale, bias_row, table, slot_rows, counts_row = start_call(
        features, slot_rows, counts_row, degree, tables, bias.reshape(1, hidden_width)
    )
    incoming = exchange(outgoing.reshape(blocks, slots, width), "blk").reshape(total, width)
    scaled = call(place_kernel, shape((rows, width), BF16), "place")(incoming, scale)
    two = moved(scaled, two_on)
    sources = (scaled, two, moved(scaled, apart_on), moved(two, other_core))
    unplace = call(unplace_kernel, shape((total, rows), BF16), "unplace", flops=10**8)(incoming)
    turned = call(transpose_kernel, shape(tiles.shape, BF16), "turn", flops=LONG)(
        tiles, after=(scaled,)
    )
    partial = tile_call(
        gather_kernel,
        shape((quarters, rows, width), BF16),
        [pltpu.VMEM((quarters * rows, width), F32)],
        "gather_tiles",
        table,
        (tiles, *sources),
        (turned, unplace),
    )
    parts = exchange(partial, "rep")
    hidden, sent = call(
        dense_kernel,
        (
            shape((rows, hidden_width), BF16),
            shape((quarters, rows + 2 * width + 16, width), BF16),
        ),
        "dense",
        (pltpu.VMEM((rows, width), BF16), pltpu.VMEM((rows, hidden_width), BF16)),
    )(parts, scale, weight, bias_row, out_grad)
    block = exchange(sent, "rep")
    own, two, near, apart, mine = tile_call(
        spread_kernel,
        (
            shape((rows, width), F32),
            shape((rows, width), F32),
            shape((rows + 2 * width, width), BF16),
            shape((rows, width), BF16),
            shape((2 * width, width), F32),
        ),
        [pltpu.VMEM((steps, rows, width), F32)],
        "spread_tiles",
        table,
        (turned, block),
    )
    near = moved(near, other_core)
    apart = moved(apart, apart_back)
    two, terms = call(
        add_kernel, (shape((rows, width), BF16), shape((2 * width, width), BF16)), "add"
    )(two, mine, near)
    added = two
    two = moved(two, two_back)
    cores = [list(range(core, blocks, 2)) for core in range(2)]
    terms = exchange(terms.reshape(blocks // 2, 4, width), "blk", cores).reshape(terms.shape)
    arrive = call(arrive_kernel, shape((rows, total), BF16), "arrive")(
        slot_rows, counts_row, after=(added,)
    )
    back = call(back_kernel, shape((blocks * (slots + 4), width), BF16), "back")(
        own, apart, two, scale, unplace, terms, after=(arrive,)
    )
    returned = exchange(back.reshape(blocks, 3, 4, width), "blk").reshape(back.shape)
    grad_features, grad_weight, grad_bias = call(
        last_kernel,
        (shape((rows, width), BF16), shape(weight.shape, F32), shape((1, hidden_width), F32)),
        "last",
    )(arrive, returned)
    return (hidden, grad_features, grad_weight, grad_bias.reshape(hidden_width))


def solution(mesh):
    in_specs = (
        P(("blk", "rep"), None),
        P(("blk", "rep"), None),
        P(("blk", "rep")),
        P(("blk", "rep"), None, None, None),
        P(("blk", "rep"), None),
        P(("blk", "rep"), None),
        P(("blk", "rep")),
        P(("blk", "rep")),
        P(),
        P(),
        P(("blk", "rep"), None),
    )
    out_specs = (P(("blk", "rep"), None), P(("blk", "rep"), None), P(), P())
    return jax.shard_map(
        on_device, mesh=mesh, in_specs=in_specs, out_specs=out_specs, check_vma=False
    )
```

```python
import jax
import jax.numpy as jnp
from jax import lax
from jax.experimental import pallas as pl
from jax.experimental.pallas import tpu as pltpu
from jax.sharding import PartitionSpec as P

BF16 = jnp.bfloat16
F32 = jnp.float32
TILE = 128
LONG = 10**11
UNUSED = 1024.0
NN = (((1,), (0,)), ((), ()))
NT = (((1,), (1,)), ((), ()))
TN = (((0,), (0,)), ((), ()))


def dot(a, b, dims=NN):
    return lax.dot_general(a, b, dims, preferred_element_type=F32)


def iota(shape, dim):
    return lax.broadcasted_iota(jnp.int32, shape, dim)


def one_hot(mask):
    return jnp.where(mask, 1.0, 0.0).astype(BF16)


def kernel_call(kernel, outs, specs, name, scratch=(), flops=10**8):
    return pl.pallas_call(
        kernel,
        out_shape=outs,
        in_specs=specs,
        scratch_shapes=list(scratch),
        compiler_params=pltpu.CompilerParams(vmem_limit_bytes=16 * 1024 * 1024),
        cost_estimate=pl.CostEstimate(flops=flops, bytes_accessed=10**6, transcendentals=0),
        name=name,
    )


def call(kernel, outs, name, scratch=(), flops=10**8):
    def run(*arrays, after=()):
        specs = [pl.BlockSpec(memory_space=pltpu.VMEM)] * len(arrays)
        specs += [pl.BlockSpec(memory_space=pl.ANY)] * len(after)
        return kernel_call(kernel, outs, specs, name, scratch, flops)(*arrays, *after)

    return run


def shape(dims, kind):
    return jax.ShapeDtypeStruct(dims, kind)


def quotient(value, divisor):
    return jnp.floor((value.astype(F32) + 0.5) * (1.0 / divisor)).astype(jnp.int32)


def as_column(row):
    return jnp.transpose(jnp.broadcast_to(row, (TILE, TILE)))


def slot_parts(send_rows, counts, rows):
    send_rows = jnp.transpose(send_rows.astype(F32)).astype(jnp.int32)
    owners, slots = send_rows.shape
    count = as_column(counts.astype(F32))[:, :slots]
    lane = iota((owners, slots), 1).astype(F32)
    key = jnp.where(lane < count, send_rows, rows)
    high = (key >> 5).astype(F32).astype(BF16)
    low = (key & 31).astype(F32).astype(BF16)
    total = owners * slots
    expand = one_hot(iota((total, owners), 0) // slots == iota((total, owners), 1))
    mine = iota((total, slots), 0) % slots == iota((total, slots), 1)
    high = jnp.where(mine, dot(expand, high) * 32.0, 0.0).astype(BF16)
    low = jnp.where(mine, dot(expand, low), 0.0).astype(BF16)
    return high, low


def start_kernel(*refs):
    out_ref, degree_ref, bias_ref, table_ref, rows_ref, counts_ref = refs[8:14]
    features_ref, *parts, sems = refs[14:]
    pairs = tuple(zip(refs[:8], (features_ref, rows_ref, counts_ref, degree_ref, *parts, bias_ref)))
    copies = [pltpu.make_async_copy(a, b, sems.at[k]) for k, (a, b) in enumerate(pairs)]
    for copy in copies:
        copy.start()
    copies[1].wait()
    copies[2].wait()
    rows = features_ref.shape[0]
    slots = rows_ref.shape[0]
    high, low = slot_parts(rows_ref[...], counts_ref[...], rows)
    ones = jnp.ones((slots, TILE), BF16)
    key = dot(high, ones) + dot(low, ones)
    lane = iota(key.shape, 1).astype(F32)
    pick = jnp.concatenate(
        [one_hot(key == lane + float(start)) for start in range(0, rows, TILE)], axis=1
    )
    copies[0].wait()
    sent = dot(pick, features_ref[...])
    out_ref[...] = jnp.where(key >= float(rows), UNUSED, sent).astype(BF16)
    for copy in copies[3:]:
        copy.wait()
    place = 0
    for part in parts:
        table_ref[place : place + part.shape[0]] = part[...]
        place += part.shape[0]
    odd = lax.rem(lax.axis_index("blk"), 2)
    table_ref[place : place + 1] = jnp.full((1, table_ref.shape[1]), odd, jnp.int32)


def start_call(features, send_rows, counts_row, degree, tables, bias_row):
    rows, width = features.shape
    total = send_rows.size
    small = (features, send_rows, counts_row, degree, *tables)
    arrays = [pltpu.with_memory_space_constraint(a, pltpu.HBM) for a in (*small, bias_row)]
    return pl.pallas_call(
        start_kernel,
        out_shape=(
            shape((total, width), BF16),
            shape(degree.shape, F32),
            shape(bias_row.shape, F32),
            shape((1 + sum(a.shape[0] for a in tables), tables[0].shape[1]), jnp.int32),
            shape(send_rows.shape, jnp.int32),
            shape(counts_row.shape, jnp.int32),
        ),
        in_specs=[pl.BlockSpec(memory_space=pltpu.HBM)] * 8,
        scratch_shapes=[pltpu.VMEM(a.shape, a.dtype) for a in (features, *tables)]
        + [pltpu.SemaphoreType.DMA((8,))],
        compiler_params=pltpu.CompilerParams(vmem_limit_bytes=8 * 1024 * 1024),
        cost_estimate=pl.CostEstimate(flops=10**8, bytes_accessed=10**6, transcendentals=0),
        name="start",
    )(*arrays)


def arrive_kernel(rows_ref, counts_ref, *refs):
    out_ref = refs[-1]
    rows = out_ref.shape[0]
    high, low = slot_parts(rows_ref[...], counts_ref[...], rows)
    ones = jnp.ones((8, rows_ref.shape[0]), BF16)
    key = dot(ones, high, NT) + dot(ones, low, NT)
    for start in range(0, key.shape[1], TILE):
        span = slice(start, start + TILE)
        out_ref[:, span] = one_hot(iota((rows, TILE), 0).astype(F32) == key[0:1, span])


def transpose_kernel(tiles_ref, *refs):
    out_ref = refs[-1]
    for t in range(tiles_ref.shape[0]):
        out_ref[t] = jnp.transpose(tiles_ref[t].astype(F32)).astype(BF16)


def used_slots(ref):
    return jnp.where(ref[...].astype(F32) < 512.0, 1.0, 0.0).astype(BF16)


def scaled_rows(degree_ref, values):
    count = values.shape[0] // TILE
    parts = [
        as_column(degree_ref[t : t + 1]) * values[t * TILE : (t + 1) * TILE] for t in range(count)
    ]
    return jnp.concatenate(parts, axis=0)


def place_kernel(incoming_ref, degree_ref, out_ref):
    rows = out_ref.shape[0]
    used = used_slots(incoming_ref)
    before = one_hot(iota((TILE, TILE), 0) < iota((TILE, TILE), 1))
    ones = jnp.ones((TILE, TILE), BF16)
    mean = jnp.full((8, TILE), 1.0 / TILE, BF16)
    offset = jnp.zeros((8, TILE), F32)
    parts = []
    for start in range(0, used.shape[0], TILE):
        here = dot(mean, used[start : start + TILE], NT)
        flags = here.astype(BF16)
        rank = jnp.where(here > 0.5, dot(flags, before) + offset, -1.0)
        offset = offset + dot(flags, ones)
        parts.append(one_hot(iota((rows, TILE), 0).astype(F32) == rank[0:1]))
    owned = dot(jnp.concatenate(parts, axis=1), incoming_ref[...])
    out_ref[...] = scaled_rows(degree_ref, owned).astype(BF16)


def unplace_kernel(incoming_ref, out_ref):
    rows = out_ref.shape[1]
    used = used_slots(incoming_ref)
    before = one_hot(iota((TILE, TILE), 1) < iota((TILE, TILE), 0))
    ones = jnp.ones((TILE, TILE), BF16)
    offset = jnp.zeros((TILE, TILE), F32)
    lane = iota((TILE, TILE), 1).astype(F32)
    for start in range(0, used.shape[0], TILE):
        here = used[start : start + TILE]
        rank = jnp.where(here.astype(F32) > 0.5, dot(before, here) + offset, -1.0)
        offset = offset + dot(ones, here)
        for column in range(0, rows, TILE):
            out_ref[start : start + TILE, column : column + TILE] = one_hot(
                rank == lane + float(column)
            )


def gather_kernel(table_ref, tiles_ref, src0, two, apart, near, *refs):
    out_ref, acc_ref = refs[-2:]
    acc_ref[...] = jnp.zeros_like(acc_ref)
    most = table_ref.shape[1]
    steps = tiles_ref.shape[0] // most
    odd = table_ref[2 * steps + 1, 0]
    for step, source in ((0, src0), (2, two), (3 - 2 * odd, apart), (1 + 2 * odd, near)):
        for k in range(most):
            col = pl.multiple_of(table_ref[steps + step, k] * TILE, TILE)
            row = pl.multiple_of(table_ref[step, k] * TILE, TILE)
            live = (k < table_ref[2 * steps, step]).astype(F32)
            prod = dot(tiles_ref[step * most + k], source[pl.ds(col, TILE), :])
            acc_ref[pl.ds(row, TILE), :] += prod * live
    quarters, rows, _ = out_ref.shape
    for q in range(quarters):
        out_ref[q] = acc_ref[q * rows : (q + 1) * rows].astype(BF16)


def dense_kernel(
    parts_ref, degree_ref, weight_ref, bias_ref, out_grad_ref, hidden_ref, out_ref, agg_ref, grad_pre_ref
):
    quarters, rows, width = parts_ref.shape
    summed = parts_ref[0].astype(F32)
    for q in range(1, quarters):
        summed = summed + parts_ref[q].astype(F32)
    for t in range(rows // TILE):
        part = slice(t * TILE, (t + 1) * TILE)
        scale = as_column(degree_ref[t : t + 1])
        agg = (scale * summed[part]).astype(BF16)
        agg_ref[part] = agg
        pre = dot(agg, weight_ref[...]) + bias_ref[...]
        sig = jax.nn.sigmoid(pre)
        hidden_ref[part] = (pre * sig).astype(BF16)
        grad_pre = (
            out_grad_ref[part].astype(F32) * (sig * (1.0 + pre * (1.0 - sig)))
        ).astype(BF16)
        grad_pre_ref[part] = grad_pre
        grad_agg = (scale * dot(grad_pre, weight_ref[...], NT)).astype(BF16)
        for q in range(quarters):
            out_ref[q, part] = grad_agg
    grad_pre = grad_pre_ref[...]
    term = dot(agg_ref[...], grad_pre, TN).astype(BF16)
    total = jnp.sum(grad_pre.astype(F32), axis=0, keepdims=True)
    high = total.astype(BF16).astype(F32)
    pieces = (high[:, :TILE], high[:, TILE:], (total - high)[:, :TILE], (total - high)[:, TILE:])
    row = iota((16, TILE), 0)
    ends = jnp.zeros((16, TILE), F32)
    for k, piece in enumerate(pieces):
        ends = jnp.where(row == k, piece, ends)
    for q in range(quarters):
        out_ref[q, rows : rows + width] = term[:, :TILE]
        out_ref[q, rows + width : rows + 2 * width] = term[:, TILE:]
        out_ref[q, rows + 2 * width :] = ends.astype(BF16)


def terms_halves(block_ref):
    quarters, all_rows, width = block_ref.shape
    rows = all_rows - 2 * width - 16
    total = block_ref[0, rows:].astype(F32)
    for q in range(1, quarters):
        total = total + block_ref[q, rows:].astype(F32)
    ends = total[2 * width :]
    half = width // 2
    lines = (4 * half, half)
    out = [jnp.zeros((4 * half, TILE), F32) for _ in range(2)]
    for k in range(4):
        if k < 2:
            piece = total[k * width : (k + 1) * width]
        else:
            bias = ends[k - 2 : k - 1] + ends[k : k + 1]
            mine = (iota((width, TILE), 1) + (k - 2) * TILE) // 2 == iota((width, TILE), 0)
            piece = jnp.where(mine, bias, 0.0)
        here = one_hot(iota(lines, 0) == 4 * iota(lines, 1) + k)
        piece = piece.astype(BF16)
        out = [out[h] + dot(here, piece[h * half : (h + 1) * half]) for h in range(2)]
    return out


def spread_kernel(table_ref, tiles_ref, block_ref, *refs):
    own_ref, two_ref, near_ref, apart_ref, mine_ref, acc_ref = refs
    acc_ref[...] = jnp.zeros_like(acc_ref)
    most = table_ref.shape[1]
    steps = tiles_ref.shape[0] // most
    col_tiles = own_ref.shape[0] // TILE
    for step in range(steps - 1, -1, -1):
        for k in range(most):
            col = pl.multiple_of(table_ref[steps + step, k] * TILE, TILE)
            quarter = table_ref[step, k] // col_tiles
            row = pl.multiple_of(table_ref[step, k] % col_tiles * TILE, TILE)
            live = (k < table_ref[2 * steps, step]).astype(F32)
            prod = dot(tiles_ref[step * most + k], block_ref[quarter, pl.ds(row, TILE), :])
            acc_ref[step, pl.ds(col, TILE), :] += prod * live
    odd = table_ref[2 * steps + 1, 0]
    own_ref[...] = acc_ref[0]
    two_ref[...] = acc_ref[2]
    rows = own_ref.shape[0]
    near_ref[:rows] = acc_ref[1 + 2 * odd].astype(BF16)
    first, second = terms_halves(block_ref)
    mine_ref[...] = jnp.where(odd == 0, first, second)
    near_ref[rows:] = jnp.where(odd == 0, second, first).astype(BF16)
    apart_ref[...] = acc_ref[3 - 2 * odd].astype(BF16)


def row_kernel(parts_ref, *refs):
    out_ref = refs[-1]
    count, width = parts_ref.shape
    pairs = jnp.sum(parts_ref[...].astype(F32).reshape(count // 8, 8, width), axis=0)
    out_ref[...] = jnp.concatenate([pairs[:4] + pairs[4:], jnp.zeros((4, width), F32)], axis=0)


def add_kernel(two_ref, mine_ref, near_ref, out_ref, terms_ref):
    rows = out_ref.shape[0]
    out_ref[...] = (two_ref[...] + near_ref[:rows].astype(F32)).astype(BF16)
    terms_ref[...] = (mine_ref[...] + near_ref[rows:].astype(F32)).astype(BF16)


def slot_of(lines, dim):
    index = iota(lines, dim)
    owner = quotient(index, 12)
    return owner, index - 12 * owner


def back_kernel(own_ref, in1, in2, degree_ref, unplace_ref, terms_ref, *refs):
    out_ref = refs[-1]
    total = own_ref[...] + in1[...].astype(F32) + in2[...].astype(F32)
    grads = scaled_rows(degree_ref, total).astype(BF16)
    slots = dot(unplace_ref[...], grads).astype(BF16)
    empty = jnp.zeros((TILE - 8, terms_ref.shape[1]), F32)
    term = jnp.concatenate([terms_ref[...], empty], axis=0).astype(BF16)
    lines = (TILE // 8 * 12, TILE)
    owner, slot = slot_of(lines, 0)
    widen = one_hot((slot < 8) & (owner * 8 + slot == iota(lines, 1)))
    ends = dot(one_hot(slot == 8 + iota(lines, 1)), term)
    for t in range(slots.shape[0] // TILE):
        group = dot(widen, slots[t * TILE : (t + 1) * TILE]) + ends
        out_ref[t * lines[0] : (t + 1) * lines[0]] = group.astype(BF16)


def last_kernel(arrive_ref, returned_ref, out_ref, weight_ref, bias_ref):
    rows = out_ref.shape[0]
    owners = TILE // 8
    lines = (TILE + 3 * owners, 12 * owners)
    owner, slot = slot_of(lines, 1)
    row = iota(lines, 0)
    wanted = (slot < 8) & (owner * 8 + slot == row)
    place = TILE + owner % 2 * (owners // 2) + owner // 2
    wanted |= ((slot == 8) & (place == row)) | ((slot == 9) & (place + owners == row))
    wanted |= ((slot == 10) & (row == TILE + 2 * owners)) | ((slot == 11) & (row == TILE + 2 * owners + 1))
    pick = one_hot(wanted)
    total = jnp.zeros((rows, TILE), F32)
    bias = jnp.zeros((owners, TILE), F32)
    for t in range(returned_ref.shape[0] // lines[1]):
        found = dot(pick, returned_ref[t * lines[1] : (t + 1) * lines[1]])
        span = slice(t * TILE, (t + 1) * TILE)
        total = total + dot(arrive_ref[:, span], found[:TILE].astype(BF16))
        for k in range(2):
            for core in range(2):
                start = TILE + (2 * k + core) * (owners // 2)
                line = core * (weight_ref.shape[0] // 2) + t * (owners // 2)
                part = found[start : start + owners // 2]
                weight_ref[line : line + owners // 2, k * TILE : (k + 1) * TILE] = part
        bias = bias + found[TILE + 2 * owners :]
    out_ref[...] = total.astype(BF16)
    bias_ref[:, :TILE] = bias[0:1]
    bias_ref[:, TILE:] = bias[1:2]


def moved(value, target):
    count = lax.axis_size("blk")
    return lax.ppermute(value, "blk", [(s, target(s) % count) for s in range(count)])


def two_on(blk):
    return blk + 2


def two_back(blk):
    return blk - 2


def apart_on(blk):
    return blk + 1 + 2 * (blk % 2)


def apart_back(blk):
    return blk - 3 + 2 * (blk % 2)


def other_core(blk):
    return blk + 1 - 2 * (blk % 2)


def exchange(value, axis, groups=None):
    return lax.all_to_all(
        value, axis, split_axis=0, concat_axis=0, axis_index_groups=groups, tiled=True
    )


def tile_call(kernel, outs, scratch, name, table, arrays, after=()):
    specs = [pl.BlockSpec(memory_space=pltpu.SMEM)]
    specs += [pl.BlockSpec(memory_space=pltpu.VMEM)] * len(arrays)
    specs += [pl.BlockSpec(memory_space=pl.ANY)] * len(after)
    return kernel_call(kernel, outs, specs, name, scratch)(table, *arrays, *after)


def on_device(
    features,
    send_rows,
    send_counts,
    tile_values,
    tile_rows,
    tile_cols,
    tile_counts,
    degree_scale,
    weight,
    bias,
    out_grad,
):
    blocks = lax.axis_size("blk")
    quarters = lax.axis_size("rep")
    rows, width = features.shape
    slots = send_rows.shape[1]
    steps, most = tile_values.shape[:2]
    hidden_width = weight.shape[1]
    total = blocks * slots
    slot_rows = send_rows.T
    counts_row = send_counts.reshape(1, blocks)
    degree = degree_scale.reshape(rows // TILE, TILE)
    tiles = tile_values.reshape(steps * most, TILE, TILE)
    tables = (tile_rows, tile_cols, tile_counts.reshape(1, steps))

    outgoing, scale, bias_row, table, slot_rows, counts_row = start_call(
        features, slot_rows, counts_row, degree, tables, bias.reshape(1, hidden_width)
    )
    incoming = exchange(outgoing.reshape(blocks, slots, width), "blk").reshape(total, width)
    scaled = call(place_kernel, shape((rows, width), BF16), "place")(incoming, scale)
    two = moved(scaled, two_on)
    sources = (scaled, two, moved(scaled, apart_on), moved(two, other_core))
    unplace = call(unplace_kernel, shape((total, rows), BF16), "unplace", flops=10**8)(incoming)
    turned = call(transpose_kernel, shape(tiles.shape, BF16), "turn", flops=LONG)(
        tiles, after=(scaled,)
    )
    partial = tile_call(
        gather_kernel,
        shape((quarters, rows, width), BF16),
        [pltpu.VMEM((quarters * rows, width), F32)],
        "gather_tiles",
        table,
        (tiles, *sources),
        (turned, unplace),
    )
    parts = exchange(partial, "rep")
    hidden, sent = call(
        dense_kernel,
        (
            shape((rows, hidden_width), BF16),
            shape((quarters, rows + 2 * width + 16, width), BF16),
        ),
        "dense",
        (pltpu.VMEM((rows, width), BF16), pltpu.VMEM((rows, hidden_width), BF16)),
    )(parts, scale, weight, bias_row, out_grad)
    block = exchange(sent, "rep")
    own, two, near, apart, mine = tile_call(
        spread_kernel,
        (
            shape((rows, width), F32),
            shape((rows, width), F32),
            shape((rows + 2 * width, width), BF16),
            shape((rows, width), BF16),
            shape((2 * width, width), F32),
        ),
        [pltpu.VMEM((steps, rows, width), F32)],
        "spread_tiles",
        table,
        (turned, block),
    )
    near = moved(near, other_core)
    apart = moved(apart, apart_back)
    two, terms = call(
        add_kernel, (shape((rows, width), BF16), shape((2 * width, width), BF16)), "add"
    )(two, mine, near)
    added = two
    two = moved(two, two_back)
    cores = [list(range(core, blocks, 2)) for core in range(2)]
    terms = exchange(terms.reshape(blocks // 2, 4, width), "blk", cores).reshape(terms.shape)
    arrive = call(arrive_kernel, shape((rows, total), BF16), "arrive")(
        slot_rows, counts_row, after=(added,)
    )
    terms = call(row_kernel, shape((8, TILE), F32), "row", flops=LONG)(terms, after=(two,))
    back = call(back_kernel, shape((blocks * (slots + 4), width), BF16), "back")(
        own, apart, two, scale, unplace, terms, after=(arrive,)
    )
    returned = exchange(back.reshape(blocks, 3, 4, width), "blk").reshape(back.shape)
    grad_features, grad_weight, grad_bias = call(
        last_kernel,
        (shape((rows, width), BF16), shape(weight.shape, F32), shape((1, hidden_width), F32)),
        "last",
    )(arrive, returned)
    return (hidden, grad_features, grad_weight, grad_bias.reshape(hidden_width))


def solution(mesh):
    in_specs = (
        P(("blk", "rep"), None),
        P(("blk", "rep"), None),
        P(("blk", "rep")),
        P(("blk", "rep"), None, None, None),
        P(("blk", "rep"), None),
        P(("blk", "rep"), None),
        P(("blk", "rep")),
        P(("blk", "rep")),
        P(),
        P(),
        P(("blk", "rep"), None),
    )
    out_specs = (P(("blk", "rep"), None), P(("blk", "rep"), None), P(), P())
    return jax.shard_map(
        on_device, mesh=mesh, in_specs=in_specs, out_specs=out_specs, check_vma=False
    )
```

```python
import jax
import jax.numpy as jnp
from jax import lax
from jax.experimental import pallas as pl
from jax.experimental.pallas import tpu as pltpu
from jax.sharding import PartitionSpec as P

BF16 = jnp.bfloat16
F32 = jnp.float32
TILE = 128
LONG = 10**11
UNUSED = 1024.0
NN = (((1,), (0,)), ((), ()))
NT = (((1,), (1,)), ((), ()))
TN = (((0,), (0,)), ((), ()))


def dot(a, b, dims=NN):
    return lax.dot_general(a, b, dims, preferred_element_type=F32)


def iota(shape, dim):
    return lax.broadcasted_iota(jnp.int32, shape, dim)


def one_hot(mask):
    return jnp.where(mask, 1.0, 0.0).astype(BF16)


def kernel_call(kernel, outs, specs, name, scratch=(), flops=10**8):
    return pl.pallas_call(
        kernel,
        out_shape=outs,
        in_specs=specs,
        scratch_shapes=list(scratch),
        compiler_params=pltpu.CompilerParams(vmem_limit_bytes=16 * 1024 * 1024),
        cost_estimate=pl.CostEstimate(flops=flops, bytes_accessed=10**6, transcendentals=0),
        name=name,
    )


def call(kernel, outs, name, scratch=(), flops=10**8):
    def run(*arrays, after=()):
        specs = [pl.BlockSpec(memory_space=pltpu.VMEM)] * len(arrays)
        specs += [pl.BlockSpec(memory_space=pl.ANY)] * len(after)
        return kernel_call(kernel, outs, specs, name, scratch, flops)(*arrays, *after)

    return run


def shape(dims, kind):
    return jax.ShapeDtypeStruct(dims, kind)


def quotient(value, divisor):
    return jnp.floor((value.astype(F32) + 0.5) * (1.0 / divisor)).astype(jnp.int32)


def as_column(row):
    return jnp.transpose(jnp.broadcast_to(row, (TILE, TILE)))


def slot_parts(send_rows, counts, rows):
    send_rows = jnp.transpose(send_rows.astype(F32)).astype(jnp.int32)
    owners, slots = send_rows.shape
    count = as_column(counts.astype(F32))[:, :slots]
    lane = iota((owners, slots), 1).astype(F32)
    key = jnp.where(lane < count, send_rows, rows)
    high = (key >> 5).astype(F32).astype(BF16)
    low = (key & 31).astype(F32).astype(BF16)
    total = owners * slots
    expand = one_hot(iota((total, owners), 0) // slots == iota((total, owners), 1))
    mine = iota((total, slots), 0) % slots == iota((total, slots), 1)
    high = jnp.where(mine, dot(expand, high) * 32.0, 0.0).astype(BF16)
    low = jnp.where(mine, dot(expand, low), 0.0).astype(BF16)
    return high, low


def start_kernel(*refs):
    out_ref, degree_ref, bias_ref, table_ref, rows_ref, counts_ref = refs[8:14]
    features_ref, *parts, sems = refs[14:]
    pairs = tuple(zip(refs[:8], (features_ref, rows_ref, counts_ref, degree_ref, *parts, bias_ref)))
    copies = [pltpu.make_async_copy(a, b, sems.at[k]) for k, (a, b) in enumerate(pairs)]
    for copy in copies:
        copy.start()
    copies[1].wait()
    copies[2].wait()
    rows = features_ref.shape[0]
    slots = rows_ref.shape[0]
    high, low = slot_parts(rows_ref[...], counts_ref[...], rows)
    ones = jnp.ones((slots, TILE), BF16)
    key = dot(high, ones) + dot(low, ones)
    lane = iota(key.shape, 1).astype(F32)
    pick = jnp.concatenate(
        [one_hot(key == lane + float(start)) for start in range(0, rows, TILE)], axis=1
    )
    copies[0].wait()
    sent = dot(pick, features_ref[...])
    out_ref[...] = jnp.where(key >= float(rows), UNUSED, sent).astype(BF16)
    for copy in copies[3:]:
        copy.wait()
    place = 0
    for part in parts:
        table_ref[place : place + part.shape[0]] = part[...]
        place += part.shape[0]
    odd = lax.rem(lax.axis_index("blk"), 2)
    table_ref[place : place + 1] = jnp.full((1, table_ref.shape[1]), odd, jnp.int32)


def start_call(features, send_rows, counts_row, degree, tables, bias_row):
    rows, width = features.shape
    total = send_rows.size
    small = (features, send_rows, counts_row, degree, *tables)
    arrays = [pltpu.with_memory_space_constraint(a, pltpu.HBM) for a in (*small, bias_row)]
    return pl.pallas_call(
        start_kernel,
        out_shape=(
            shape((total, width), BF16),
            shape(degree.shape, F32),
            shape(bias_row.shape, F32),
            shape((1 + sum(a.shape[0] for a in tables), tables[0].shape[1]), jnp.int32),
            shape(send_rows.shape, jnp.int32),
            shape(counts_row.shape, jnp.int32),
        ),
        in_specs=[pl.BlockSpec(memory_space=pltpu.HBM)] * 8,
        scratch_shapes=[pltpu.VMEM(a.shape, a.dtype) for a in (features, *tables)]
        + [pltpu.SemaphoreType.DMA((8,))],
        compiler_params=pltpu.CompilerParams(vmem_limit_bytes=8 * 1024 * 1024),
        cost_estimate=pl.CostEstimate(flops=10**8, bytes_accessed=10**6, transcendentals=0),
        name="start",
    )(*arrays)


def arrive_kernel(rows_ref, counts_ref, *refs):
    out_ref = refs[-1]
    rows = out_ref.shape[0]
    high, low = slot_parts(rows_ref[...], counts_ref[...], rows)
    ones = jnp.ones((8, rows_ref.shape[0]), BF16)
    key = dot(ones, high, NT) + dot(ones, low, NT)
    for start in range(0, key.shape[1], TILE):
        span = slice(start, start + TILE)
        out_ref[:, span] = one_hot(iota((rows, TILE), 0).astype(F32) == key[0:1, span])


def transpose_kernel(tiles_ref, *refs):
    out_ref = refs[-1]
    for t in range(tiles_ref.shape[0]):
        out_ref[t] = jnp.transpose(tiles_ref[t].astype(F32)).astype(BF16)


def used_slots(ref):
    return jnp.where(ref[...].astype(F32) < 512.0, 1.0, 0.0).astype(BF16)


def scaled_rows(degree_ref, values):
    count = values.shape[0] // TILE
    parts = [
        as_column(degree_ref[t : t + 1]) * values[t * TILE : (t + 1) * TILE] for t in range(count)
    ]
    return jnp.concatenate(parts, axis=0)


def place_kernel(incoming_ref, degree_ref, out_ref):
    rows = out_ref.shape[0]
    used = used_slots(incoming_ref)
    before = one_hot(iota((TILE, TILE), 0) < iota((TILE, TILE), 1))
    ones = jnp.ones((TILE, TILE), BF16)
    mean = jnp.full((8, TILE), 1.0 / TILE, BF16)
    offset = jnp.zeros((8, TILE), F32)
    parts = []
    for start in range(0, used.shape[0], TILE):
        here = dot(mean, used[start : start + TILE], NT)
        flags = here.astype(BF16)
        rank = jnp.where(here > 0.5, dot(flags, before) + offset, -1.0)
        offset = offset + dot(flags, ones)
        parts.append(one_hot(iota((rows, TILE), 0).astype(F32) == rank[0:1]))
    owned = dot(jnp.concatenate(parts, axis=1), incoming_ref[...])
    out_ref[...] = scaled_rows(degree_ref, owned).astype(BF16)


def unplace_kernel(incoming_ref, out_ref):
    rows = out_ref.shape[1]
    used = used_slots(incoming_ref)
    before = one_hot(iota((TILE, TILE), 1) < iota((TILE, TILE), 0))
    ones = jnp.ones((TILE, TILE), BF16)
    offset = jnp.zeros((TILE, TILE), F32)
    lane = iota((TILE, TILE), 1).astype(F32)
    for start in range(0, used.shape[0], TILE):
        here = used[start : start + TILE]
        rank = jnp.where(here.astype(F32) > 0.5, dot(before, here) + offset, -1.0)
        offset = offset + dot(ones, here)
        for column in range(0, rows, TILE):
            out_ref[start : start + TILE, column : column + TILE] = one_hot(
                rank == lane + float(column)
            )


def gather_kernel(table_ref, tiles_ref, src0, two, apart, near, *refs):
    out_ref, acc_ref = refs[-2:]
    acc_ref[...] = jnp.zeros_like(acc_ref)
    most = table_ref.shape[1]
    steps = tiles_ref.shape[0] // most
    odd = table_ref[2 * steps + 1, 0]
    for step, source in ((0, src0), (2, two), (3 - 2 * odd, apart), (1 + 2 * odd, near)):
        for k in range(most):
            col = pl.multiple_of(table_ref[steps + step, k] * TILE, TILE)
            row = pl.multiple_of(table_ref[step, k] * TILE, TILE)
            live = (k < table_ref[2 * steps, step]).astype(F32)
            prod = dot(tiles_ref[step * most + k], source[pl.ds(col, TILE), :])
            acc_ref[pl.ds(row, TILE), :] += prod * live
    quarters, rows, _ = out_ref.shape
    for q in range(quarters):
        out_ref[q] = acc_ref[q * rows : (q + 1) * rows].astype(BF16)


def dense_kernel(
    parts_ref, degree_ref, weight_ref, bias_ref, out_grad_ref, hidden_ref, out_ref, agg_ref, grad_pre_ref
):
    quarters, rows, width = parts_ref.shape
    summed = parts_ref[0].astype(F32)
    for q in range(1, quarters):
        summed = summed + parts_ref[q].astype(F32)
    for t in range(rows // TILE):
        part = slice(t * TILE, (t + 1) * TILE)
        scale = as_column(degree_ref[t : t + 1])
        agg = (scale * summed[part]).astype(BF16)
        agg_ref[part] = agg
        pre = dot(agg, weight_ref[...]) + bias_ref[...]
        sig = jax.nn.sigmoid(pre)
        hidden_ref[part] = (pre * sig).astype(BF16)
        grad_pre = (
            out_grad_ref[part].astype(F32) * (sig * (1.0 + pre * (1.0 - sig)))
        ).astype(BF16)
        grad_pre_ref[part] = grad_pre
        grad_agg = (scale * dot(grad_pre, weight_ref[...], NT)).astype(BF16)
        for q in range(quarters):
            out_ref[q, part] = grad_agg
    grad_pre = grad_pre_ref[...]
    term = dot(agg_ref[...], grad_pre, TN).astype(BF16)
    total = jnp.sum(grad_pre.astype(F32), axis=0, keepdims=True)
    high = total.astype(BF16).astype(F32)
    pieces = (high[:, :TILE], high[:, TILE:], (total - high)[:, :TILE], (total - high)[:, TILE:])
    row = iota((16, TILE), 0)
    ends = jnp.zeros((16, TILE), F32)
    for k, piece in enumerate(pieces):
        ends = jnp.where(row == k, piece, ends)
    for q in range(quarters):
        out_ref[q, rows : rows + width] = term[:, :TILE]
        out_ref[q, rows + width : rows + 2 * width] = term[:, TILE:]
        out_ref[q, rows + 2 * width :] = ends.astype(BF16)


def terms_halves(block_ref):
    quarters, all_rows, width = block_ref.shape
    rows = all_rows - 2 * width - 16
    total = block_ref[0, rows:].astype(F32)
    for q in range(1, quarters):
        total = total + block_ref[q, rows:].astype(F32)
    ends = total[2 * width :]
    half = width // 2
    lines = (4 * half, half)
    out = [jnp.zeros((4 * half, TILE), F32) for _ in range(2)]
    for k in range(4):
        if k < 2:
            piece = total[k * width : (k + 1) * width]
        else:
            bias = ends[k - 2 : k - 1] + ends[k : k + 1]
            mine = (iota((width, TILE), 1) + (k - 2) * TILE) // 2 == iota((width, TILE), 0)
            piece = jnp.where(mine, bias, 0.0)
        here = one_hot(iota(lines, 0) == 4 * iota(lines, 1) + k)
        piece = piece.astype(BF16)
        out = [out[h] + dot(here, piece[h * half : (h + 1) * half]) for h in range(2)]
    return out


def spread_kernel(table_ref, tiles_ref, block_ref, *refs):
    own_ref, two_ref, near_ref, apart_ref, mine_ref, acc_ref = refs
    acc_ref[...] = jnp.zeros_like(acc_ref)
    most = table_ref.shape[1]
    steps = tiles_ref.shape[0] // most
    col_tiles = own_ref.shape[0] // TILE
    for step in range(steps - 1, -1, -1):
        for k in range(most):
            col = pl.multiple_of(table_ref[steps + step, k] * TILE, TILE)
            quarter = table_ref[step, k] // col_tiles
            row = pl.multiple_of(table_ref[step, k] % col_tiles * TILE, TILE)
            live = (k < table_ref[2 * steps, step]).astype(F32)
            prod = dot(tiles_ref[step * most + k], block_ref[quarter, pl.ds(row, TILE), :])
            acc_ref[step, pl.ds(col, TILE), :] += prod * live
    odd = table_ref[2 * steps + 1, 0]
    own_ref[...] = acc_ref[0]
    two_ref[...] = acc_ref[2]
    rows = own_ref.shape[0]
    near_ref[:rows] = acc_ref[1 + 2 * odd].astype(BF16)
    first, second = terms_halves(block_ref)
    mine_ref[...] = jnp.where(odd == 0, first, second)
    near_ref[rows:] = jnp.where(odd == 0, second, first).astype(BF16)
    apart_ref[...] = acc_ref[3 - 2 * odd].astype(BF16)


def row_kernel(parts_ref, *refs):
    out_ref = refs[-1]
    count, width = parts_ref.shape
    pairs = jnp.sum(parts_ref[...].astype(F32).reshape(count // 8, 8, width), axis=0)
    out_ref[...] = jnp.concatenate([pairs[:4] + pairs[4:], jnp.zeros((4, width), F32)], axis=0)


def add_kernel(two_ref, mine_ref, near_ref, out_ref, terms_ref):
    rows = out_ref.shape[0]
    out_ref[...] = (two_ref[...] + near_ref[:rows].astype(F32)).astype(BF16)
    terms_ref[...] = (mine_ref[...] + near_ref[rows:].astype(F32)).astype(BF16)


def slot_of(lines, dim):
    index = iota(lines, dim)
    owner = quotient(index, 12)
    return owner, index - 12 * owner


def back_kernel(own_ref, in1, in2, degree_ref, unplace_ref, terms_ref, *refs):
    out_ref = refs[-1]
    total = own_ref[...] + in1[...].astype(F32) + in2[...].astype(F32)
    grads = scaled_rows(degree_ref, total).astype(BF16)
    slots = dot(unplace_ref[...], grads).astype(BF16)
    empty = jnp.zeros((TILE - 8, terms_ref.shape[1]), F32)
    term = jnp.concatenate([terms_ref[...], empty], axis=0).astype(BF16)
    lines = (TILE // 8 * 12, TILE)
    owner, slot = slot_of(lines, 0)
    widen = one_hot((slot < 8) & (owner * 8 + slot == iota(lines, 1)))
    ends = dot(one_hot(slot == 8 + iota(lines, 1)), term)
    for t in range(slots.shape[0] // TILE):
        group = dot(widen, slots[t * TILE : (t + 1) * TILE]) + ends
        out_ref[t * lines[0] : (t + 1) * lines[0]] = group.astype(BF16)


def last_kernel(arrive_ref, returned_ref, out_ref, weight_ref, bias_ref):
    rows = out_ref.shape[0]
    owners = TILE // 8
    lines = (TILE + 3 * owners, 12 * owners)
    owner, slot = slot_of(lines, 1)
    row = iota(lines, 0)
    wanted = (slot < 8) & (owner * 8 + slot == row)
    place = TILE + owner % 2 * (owners // 2) + owner // 2
    wanted |= ((slot == 8) & (place == row)) | ((slot == 9) & (place + owners == row))
    wanted |= ((slot == 10) & (row == TILE + 2 * owners)) | ((slot == 11) & (row == TILE + 2 * owners + 1))
    pick = one_hot(wanted)
    total = jnp.zeros((rows, TILE), F32)
    bias = jnp.zeros((owners, TILE), F32)
    for t in range(returned_ref.shape[0] // lines[1]):
        found = dot(pick, returned_ref[t * lines[1] : (t + 1) * lines[1]])
        span = slice(t * TILE, (t + 1) * TILE)
        total = total + dot(arrive_ref[:, span], found[:TILE].astype(BF16))
        for k in range(2):
            for core in range(2):
                start = TILE + (2 * k + core) * (owners // 2)
                line = core * (weight_ref.shape[0] // 2) + t * (owners // 2)
                part = found[start : start + owners // 2]
                weight_ref[line : line + owners // 2, k * TILE : (k + 1) * TILE] = part
        bias = bias + found[TILE + 2 * owners :]
    out_ref[...] = total.astype(BF16)
    bias_ref[:, :TILE] = bias[0:1]
    bias_ref[:, TILE:] = bias[1:2]


def moved(value, target):
    count = lax.axis_size("blk")
    return lax.ppermute(value, "blk", [(s, target(s) % count) for s in range(count)])


def two_on(blk):
    return blk + 2


def two_back(blk):
    return blk - 2


def apart_on(blk):
    return blk + 1 + 2 * (blk % 2)


def apart_back(blk):
    return blk - 3 + 2 * (blk % 2)


def other_core(blk):
    return blk + 1 - 2 * (blk % 2)


def exchange(value, axis, groups=None):
    return lax.all_to_all(
        value, axis, split_axis=0, concat_axis=0, axis_index_groups=groups, tiled=True
    )


def tile_call(kernel, outs, scratch, name, table, arrays, after=()):
    specs = [pl.BlockSpec(memory_space=pltpu.SMEM)]
    specs += [pl.BlockSpec(memory_space=pltpu.VMEM)] * len(arrays)
    specs += [pl.BlockSpec(memory_space=pl.ANY)] * len(after)
    return kernel_call(kernel, outs, specs, name, scratch)(table, *arrays, *after)


def on_device(
    features,
    send_rows,
    send_counts,
    tile_values,
    tile_rows,
    tile_cols,
    tile_counts,
    degree_scale,
    weight,
    bias,
    out_grad,
):
    blocks = lax.axis_size("blk")
    quarters = lax.axis_size("rep")
    rows, width = features.shape
    slots = send_rows.shape[1]
    steps, most = tile_values.shape[:2]
    hidden_width = weight.shape[1]
    total = blocks * slots
    slot_rows = send_rows.T
    counts_row = send_counts.reshape(1, blocks)
    degree = degree_scale.reshape(rows // TILE, TILE)
    tiles = tile_values.reshape(steps * most, TILE, TILE)
    tables = (tile_rows, tile_cols, tile_counts.reshape(1, steps))

    outgoing, scale, bias_row, table, slot_rows, counts_row = start_call(
        features, slot_rows, counts_row, degree, tables, bias.reshape(1, hidden_width)
    )
    incoming = exchange(outgoing.reshape(blocks, slots, width), "blk").reshape(total, width)
    scaled = call(place_kernel, shape((rows, width), BF16), "place")(incoming, scale)
    two = moved(scaled, two_on)
    sources = (scaled, two, moved(scaled, apart_on), moved(two, other_core))
    unplace = call(unplace_kernel, shape((total, rows), BF16), "unplace", flops=10**8)(incoming)
    turned = call(transpose_kernel, shape(tiles.shape, BF16), "turn", flops=LONG)(
        tiles, after=(scaled,)
    )
    partial = tile_call(
        gather_kernel,
        shape((quarters, rows, width), BF16),
        [pltpu.VMEM((quarters * rows, width), F32)],
        "gather_tiles",
        table,
        (tiles, *sources),
        (turned, unplace),
    )
    parts = exchange(partial, "rep")
    hidden, sent = call(
        dense_kernel,
        (
            shape((rows, hidden_width), BF16),
            shape((quarters, rows + 2 * width + 16, width), BF16),
        ),
        "dense",
        (pltpu.VMEM((rows, width), BF16), pltpu.VMEM((rows, hidden_width), BF16)),
    )(parts, scale, weight, bias_row, out_grad)
    block = exchange(sent, "rep")
    own, two, near, apart, mine = tile_call(
        spread_kernel,
        (
            shape((rows, width), F32),
            shape((rows, width), F32),
            shape((rows + 2 * width, width), BF16),
            shape((rows, width), BF16),
            shape((2 * width, width), F32),
        ),
        [pltpu.VMEM((steps, rows, width), F32)],
        "spread_tiles",
        table,
        (turned, block),
    )
    near = moved(near, other_core)
    apart = moved(apart, apart_back)
    two, terms = call(
        add_kernel, (shape((rows, width), BF16), shape((2 * width, width), BF16)), "add"
    )(two, mine, near)
    added = two
    two = moved(two, two_back)
    cores = [list(range(core, blocks, 2)) for core in range(2)]
    terms = exchange(terms.reshape(blocks // 2, 4, width), "blk", cores).reshape(terms.shape)
    arrive = call(arrive_kernel, shape((rows, total), BF16), "arrive")(
        slot_rows, counts_row, after=(added,)
    )
    terms = call(row_kernel, shape((8, TILE), F32), "row", flops=LONG)(terms, after=(apart,))
    back = call(back_kernel, shape((blocks * (slots + 4), width), BF16), "back")(
        own, apart, two, scale, unplace, terms, after=(arrive,)
    )
    returned = exchange(back.reshape(blocks, 3, 4, width), "blk").reshape(back.shape)
    grad_features, grad_weight, grad_bias = call(
        last_kernel,
        (shape((rows, width), BF16), shape(weight.shape, F32), shape((1, hidden_width), F32)),
        "last",
    )(arrive, returned)
    return (hidden, grad_features, grad_weight, grad_bias.reshape(hidden_width))


def solution(mesh):
    in_specs = (
        P(("blk", "rep"), None),
        P(("blk", "rep"), None),
        P(("blk", "rep")),
        P(("blk", "rep"), None, None, None),
        P(("blk", "rep"), None),
        P(("blk", "rep"), None),
        P(("blk", "rep")),
        P(("blk", "rep")),
        P(),
        P(),
        P(("blk", "rep"), None),
    )
    out_specs = (P(("blk", "rep"), None), P(("blk", "rep"), None), P(), P())
    return jax.shard_map(
        on_device, mesh=mesh, in_specs=in_specs, out_specs=out_specs, check_vma=False
    )
```
